32 devices in a mesh: dp: 16 (over z, y, core), tensor: 2 (over x).
Axes of the slice: x: 2, y: 2, z: 4, core: 2. Of those that a mesh axis runs over, the one named last changes fastest.
Arguments:
- tokens: bfloat16 [16384, 1024], P(('dp', 'tensor')), may hold values from -6 to 6
- gains: bfloat16 [2, 1024], P(None, ('dp', 'tensor')), may hold values from 0.5 to 1.5
- w_zx: bfloat16 [1024, 2, 1536], P('dp', None, 'tensor'), may hold values from -0.1875 to 0.1875
- w_bc: bfloat16 [1024, 256], P(('dp', 'tensor')), may hold values from -0.1875 to 0.1875
- w_dt: bfloat16 [1024, 24], P('dp', 'tensor'), may hold values from -0.1875 to 0.1875
- conv_x: float32 [5, 1536], P(None, 'tensor'), may hold values from -3 to 3
- conv_bc: float32 [5, 256], replicated, may hold values from -3 to 3
- head_params: float32 [3, 24], P(None, 'tensor'), may hold values from -6 to 2.5, as said below
- w_mo: bfloat16 [1536, 1024], P('tensor', 'dp'), may hold values from -0.4375 to 0.4375
- w_q: bfloat16 [1024, 512], P('dp', 'tensor'), may hold values from -0.1875 to 0.1875
- w_kv: bfloat16 [1024, 2, 128], P('dp', None, 'tensor'), may hold values from -0.1875 to 0.1875
- w_ao: bfloat16 [512, 1024], P('tensor', 'dp'), may hold values from -2 to 2
- w_gu: bfloat16 [1024, 2, 2048], P('dp', None, 'tensor'), may hold values from -0.1875 to 0.1875
- w_down: bfloat16 [2048, 1024], P('tensor', 'dp'), may hold values from -0.25 to 0.25
- cotangent: bfloat16 [16384, 1024], P(('dp', 'tensor')), may hold values from -6 to 6
Outputs:
- layer_out: bfloat16 [16384, 1024], P(('dp', 'tensor'))
- input_grad: bfloat16 [16384, 1024], P(('dp', 'tensor'))
- grad_gains: float32 [2, 1024], P(None, ('dp', 'tensor'))
- grad_zx: float32 [1024, 2, 1536], P('dp', None, 'tensor')
- grad_bc: float32 [1024, 256], P(('dp', 'tensor'))
- grad_dt: float32 [1024, 24], P('dp', 'tensor')
- grad_conv_x: float32 [5, 1536], P(None, 'tensor')
- grad_conv_bc: float32 [5, 256], replicated
- grad_head: float32 [3, 24], P(None, 'tensor')
- grad_mo: float32 [1536, 1024], P('tensor', 'dp')
- grad_q: float32 [1024, 512], P('dp', 'tensor')
- grad_kv: float32 [1024, 2, 128], P('dp', None, 'tensor')
- grad_ao: float32 [512, 1024], P('tensor', 'dp')
- grad_gu: float32 [1024, 2, 2048], P('dp', None, 'tensor')
- grad_down: float32 [2048, 1024], P('tensor', 'dp')
The draws below stay inside these ranges and needn't reach their ends.
Inputs may be any that keep to these rules, and one draw needn't show every extreme that they name: `head_params`: row 0 holds each head's time step bias, row 1 the logarithm of its decay rate, row 2 its skip coefficient.
All inputs are finite; a program needn't handle non-finite values.
Results may differ from the reference program's by a relative error of at most 0.018.
Values may be sent and summed in bfloat16 or wider, within the bound.
No kernel may reach another device: no remote copies, remote signals or barrier semaphores. Data moves between devices by JAX's collectives and lax.ppermute only.
A program may use at most 192 MiB of HBM per device.

```python
import math
import jax
import jax.numpy as jnp
from jax import lax

D = 1024
FF = 2048
HM = 24
P_SIZE = 64
N = 128
K = 4
HQ = 8
HK = 2
LEN = 1024
QROWS = 512
SBLOCK = 128
DI = 1536
TOKENS = 16384


def draw_head_params(key, part):
    key = jax.random.fold_in(key, 7)
    subkeys = jax.random.split(key, 3)
    step_bias = jax.random.uniform(subkeys[0], (HM,), jnp.float32, -6.0, -2.0)
    log_rate = jax.random.uniform(subkeys[1], (HM,), jnp.float32, 0.0, 2.5)
    skip_gain = jax.random.uniform(subkeys[2], (HM,), jnp.float32, 0.5, 1.5)
    return jnp.stack([step_bias, log_rate, skip_gain], axis=0)


def spiked(drawn, stream_key, source, target, blocks, factor):
    def block_of(axis_at):
        return (jnp.arange(drawn.shape[axis_at]) // (drawn.shape[axis_at] // blocks)).reshape((-1,) + (1,) * (drawn.ndim - 1 - axis_at))

    one_side = jax.random.permutation(stream_key, blocks)[block_of(target)]
    second = (block_of(target) + blocks // 2) % blocks
    return jnp.where((block_of(source) == one_side) | (block_of(source) == second), factor * drawn, drawn)


def levels(rng, dims, cuts, low, high):
    def one(position, shards_of):
        steps = jax.random.uniform(jax.random.fold_in(jax.random.fold_in(rng, 6), position), (shards_of,), jnp.float32, low / len(cuts), high / len(cuts))
        return jnp.repeat(jnp.exp(steps), dims[position] // shards_of).reshape((-1,) + (1,) * (len(dims) - position - 1))

    gain = one(*cuts[0])
    for cut in cuts[1:]:
        gain = gain * one(*cut)
    return gain


def bell_draw(key, shape, scale, reach, shards=(), held_as=jnp.bfloat16):
    gain = levels(key, shape, shards, -0.22, 0.18) if shards else 1.0
    drawn = jax.random.normal(key, shape, jnp.float32) * scale * gain
    return jnp.minimum(jnp.maximum(drawn, -reach), reach).astype(held_as)


def gaussian_with(rng, extent, deviation, most, cuts, heavy, held_as=jnp.bfloat16):
    drawn = deviation * jax.random.normal(rng, extent, jnp.float32)
    if cuts:
        drawn = drawn * levels(rng, extent, cuts, -0.22, 0.18)
    return jnp.clip(spiked(drawn, jax.random.fold_in(rng, 3), *heavy), -most, most).astype(held_as)


def setup_inputs(seed: int = 0) -> dict:
    key_of = jax.random.split(jax.random.key(seed), 16)
    tokens = gaussian_with(key_of[0], (TOKENS, D), 1.0, 6.0, ((0, 32),), (0, 1, 32, 2.75))
    gains = jnp.clip(1.0 + 0.1 * jax.random.normal(key_of[1], (2, D), jnp.float32), 0.5, 1.5).astype(jnp.bfloat16)
    w_zx = bell_draw(key_of[2], (D, 2, DI), D ** -0.5, 0.1875, ((0, 16), (2, 2)))
    w_bc = bell_draw(key_of[3], (D, 2 * N), D ** -0.5, 0.1875, ((0, 32),))
    w_dt = bell_draw(key_of[4], (D, HM), D ** -0.5, 0.1875, ((0, 16), (1, 2)))
    conv_x = bell_draw(key_of[5], (K + 1, DI), K ** -0.5, 3.0, ((1, 2),), jnp.float32)
    conv_bc = bell_draw(key_of[6], (K + 1, 2 * N), K ** -0.5, 3.0, (), jnp.float32)
    head_params = draw_head_params(jax.random.fold_in(key_of[15], 71), 0)
    w_mo = bell_draw(key_of[8], (DI, D), (DI // 8) ** -0.5, 0.4375, ((0, 2), (1, 16)))
    w_q = bell_draw(key_of[9], (D, HQ * P_SIZE), D ** -0.5, 0.1875, ((0, 16), (1, 2)))
    w_kv = bell_draw(key_of[10], (D, 2, HK * P_SIZE), D ** -0.5, 0.1875, ((0, 16), (2, 2)))
    w_ao = bell_draw(key_of[11], (HQ * P_SIZE, D), (HQ * P_SIZE // 64) ** -0.5, 2.0, ((0, 2), (1, 16)))
    w_gu = bell_draw(key_of[12], (D, 2, FF), D ** -0.5, 0.1875, ((0, 16), (2, 2)))
    w_down = bell_draw(key_of[13], (FF, D), (FF // 4) ** -0.5, 0.25, ((0, 2), (1, 16)))
    cotangent = gaussian_with(key_of[14], (TOKENS, D), 1.0, 6.0, ((0, 32),), (0, 1, 32, 2.75))
    return dict(tokens=tokens, gains=gains, w_zx=w_zx, w_bc=w_bc, w_dt=w_dt, conv_x=conv_x, conv_bc=conv_bc, head_params=head_params, w_mo=w_mo, w_q=w_q, w_kv=w_kv, w_ao=w_ao, w_gu=w_gu, w_down=w_down, cotangent=cotangent)


highest = lax.Precision.HIGHEST
epsilon = 1e-05
rope_base = 100000000000.0
masked_score = -1e+30

@jax.custom_vjp
def low(v):
    return lax.optimization_barrier(v.astype(jnp.bfloat16)).astype(jnp.float32)

@jax.custom_vjp
def low_back(v):
    return v

def low_keep(v):
    return (low(v), None)

def low_pass(kept, grad):
    return (grad,)

def back_keep(v):
    return (v, None)

def back_low(kept, grad):
    return (low(grad),)
low.defvjp(low_keep, low_pass)
low_back.defvjp(back_keep, back_low)

def matmul(left, right):
    return jnp.dot(left, right, precision=highest, preferred_element_type=jnp.float32)

def normalize(values, gain_row):
    inverse_rms = lax.rsqrt(lax.optimization_barrier(jnp.mean(values * values, axis=-1, keepdims=True)) + epsilon)
    return values * inverse_rms * gain_row

def rotary(values):
    length, head_count, head_size = values.shape
    half_size = head_size // 2
    frequency = jnp.exp(jnp.arange(half_size, dtype=jnp.float32) * (-2.0 * math.log(rope_base) / head_size))
    angles = jnp.arange(length, dtype=jnp.float32)[:, None] * frequency[None, :]
    cosine = jnp.cos(angles)[:, None, :]
    sine_tab = jnp.sin(angles)[:, None, :]
    first_half = values[..., :half_size]
    second = values[..., half_size:]
    return jnp.concatenate([first_half * cosine - second * sine_tab, second * cosine + first_half * sine_tab], axis=-1)

def attend(queries, keys_in, values_in):
    length, head_count, head_size = queries.shape
    kv_heads = keys_in.shape[1]
    group_size = head_count // kv_heads
    query_rot = low(rotary(queries)).reshape(length, kv_heads, group_size, head_size)
    key_rot = low(rotary(keys_in))
    value_low = low(values_in)
    columns = jnp.arange(length, dtype=jnp.int32)

    def score_block(block_start):
        query_block = lax.dynamic_slice_in_dim(query_rot, block_start, QROWS, 0)
        scores = jnp.einsum('qhgp,khp->hgqk', query_block, key_rot, precision=highest) * head_size ** (-0.5)
        scores = low_back(scores)
        row_ids = block_start + jnp.arange(QROWS, dtype=jnp.int32)
        causal = row_ids[:, None] >= columns[None, :]
        scores = jnp.where(causal, scores, masked_score)
        row_max = lax.optimization_barrier(jnp.max(scores, axis=-1, keepdims=True))
        weights = jnp.exp(scores - row_max)
        probabilities = weights / lax.optimization_barrier(jnp.sum(weights, axis=-1, keepdims=True))
        return jnp.einsum('hgqk,khp->qhgp', low(probabilities), value_low, precision=highest)
    starts = (jnp.arange(length // QROWS, dtype=jnp.int32) * QROWS).astype(jnp.int32)
    blocks = lax.map(jax.checkpoint(score_block), starts)
    return blocks.reshape(length, head_count * head_size)

def convolve(values, tap_table):
    tap_count = tap_table.shape[0] - 1
    length = values.shape[0]
    padded = jnp.concatenate([jnp.zeros((tap_count - 1, values.shape[1]), jnp.float32), values], axis=0)
    summed = tap_table[tap_count][None, :] + padded[0:length] * tap_table[0][None, :]
    for offset in range(1, tap_count):
        summed = summed + padded[offset:offset + length] * tap_table[offset][None, :]
    return summed

def mamba_mix(x_inner, b_and_c, step_raw, gate_z, conv_x, conv_bc, head_params):
    length = x_inner.shape[0]
    head_count = step_raw.shape[1]
    head_size = x_inner.shape[1] // head_count
    state_size = b_and_c.shape[1] // 2
    x_conv = jax.nn.silu(convolve(x_inner, conv_x)).reshape(length, head_count, head_size)
    bc_conv = jax.nn.silu(convolve(b_and_c, conv_bc))
    step_size = jax.nn.softplus(step_raw + head_params[0][None, :])
    decay_rate = step_size * (-jnp.exp(head_params[1]))[None, :]
    blocks = length // SBLOCK
    lower_mask = jnp.arange(SBLOCK)[:, None] >= jnp.arange(SBLOCK)[None, :]

    def scan_block(carried, pieces):
        x_block, b_block, c_block, step_block, decay_block = pieces
        cumulative = jnp.cumsum(decay_block, axis=0)
        spread = jnp.where(lower_mask[:, :, None], cumulative[:, None, :] - cumulative[None, :, :], masked_score)
        inner_cb = jnp.dot(c_block, b_block.T, precision=highest)
        mixing = jnp.exp(spread) * inner_cb[:, :, None] * step_block[None, :, :]
        local_out = jnp.einsum('tsh,shp->thp', mixing, x_block, precision=highest)
        carried_out = jnp.einsum('tn,hpn->thp', c_block, carried, precision=highest) * jnp.exp(cumulative)[:, :, None]
        tail_weight = jnp.exp(cumulative[-1][None, :] - cumulative) * step_block
        fresh_state = jnp.einsum('sh,shp,sn->hpn', tail_weight, x_block, b_block, precision=highest)
        updated = carried * jnp.exp(cumulative[-1])[:, None, None] + fresh_state
        return (updated, local_out + carried_out)
    pieces = (x_conv.reshape(blocks, SBLOCK, head_count, head_size), bc_conv[:, :state_size].reshape(blocks, SBLOCK, state_size), bc_conv[:, state_size:].reshape(blocks, SBLOCK, state_size), step_size.reshape(blocks, SBLOCK, head_count), decay_rate.reshape(blocks, SBLOCK, head_count))
    initial = jnp.zeros((head_count, head_size, state_size), jnp.float32)
    final_state, outputs = lax.scan(jax.checkpoint(scan_block), initial, pieces)
    mixed = outputs.reshape(length, head_count, head_size) + head_params[2][None, :, None] * x_conv
    return mixed.reshape(length, head_count * head_size) * jax.nn.silu(gate_z)

def layer_sequence(seq_in, params):
    gains, w_zx, w_bc, w_dt, conv_x, conv_bc, head_params, w_mo, w_q, w_kv, w_ao, w_gu, w_down = params
    length = seq_in.shape[0]
    normed = low(normalize(seq_in, gains[0]))
    zx_proj = low_back(jnp.einsum('td,dkc->tkc', normed, w_zx, precision=highest))
    bc_proj = low_back(matmul(normed, w_bc))
    step_proj = low_back(matmul(normed, w_dt))
    gated = mamba_mix(zx_proj[:, 1], bc_proj, step_proj, zx_proj[:, 0], conv_x, conv_bc, head_params)
    query_proj = low_back(matmul(normed, w_q))
    kv_proj = low_back(jnp.einsum('td,dkc->tkc', normed, w_kv, precision=highest))
    attended = attend(query_proj.reshape(length, -1, P_SIZE), kv_proj[:, 0].reshape(length, -1, P_SIZE), kv_proj[:, 1].reshape(length, -1, P_SIZE))
    branch = matmul(low(gated), w_mo) + matmul(low(attended), w_ao)
    hidden_one = seq_in + low_back(branch)
    normed_two = low(normalize(hidden_one, gains[1]))
    gate_up = low_back(jnp.einsum('td,dkc->tkc', normed_two, w_gu, precision=highest))
    activated = low(jax.nn.silu(gate_up[:, 0]) * gate_up[:, 1])
    return hidden_one + low_back(matmul(activated, w_down))

def reference(tokens, gains, w_zx, w_bc, w_dt, conv_x, conv_bc, head_params, w_mo, w_q, w_kv, w_ao, w_gu, w_down, cotangent):
    params = tuple((argument.astype(jnp.float32) for argument in (gains, w_zx, w_bc, w_dt, conv_x, conv_bc, head_params, w_mo, w_q, w_kv, w_ao, w_gu, w_down)))
    sequences = tokens.astype(jnp.float32).reshape(-1, LEN, D)

    def forward(seq_all, weights):
        return lax.map(jax.checkpoint(lambda seq_one: layer_sequence(seq_one, weights)), seq_all)
    outputs, pullback = jax.vjp(forward, sequences, params)
    seq_grad, grads = pullback(cotangent.astype(jnp.float32).reshape(-1, LEN, D))
    return (outputs.reshape(-1, D).astype(jnp.bfloat16), seq_grad.reshape(-1, D).astype(jnp.bfloat16), grads[0], grads[1], grads[2], grads[3], grads[4], grads[5], grads[6], grads[7], grads[8], grads[9], grads[10], grads[11], grads[12])
```

```python
import math

import jax
import jax.numpy as jnp
from jax import lax
from jax.experimental import pallas as pl
from jax.experimental.pallas import tpu as pltpu
from jax.sharding import PartitionSpec as P

P_SIZE = 64
LEN = 1024
CHUNK = 128
LANES = 128
QBLOCK = 256
HEAD_ROWS = 16

highest = lax.Precision.HIGHEST
epsilon = 1e-05
rope_base = 100000000000.0
masked_score = -1e30
f32 = jnp.float32
bf16 = jnp.bfloat16

NN = (((1,), (0,)), ((), ()))
NT = (((1,), (1,)), ((), ()))
TN = (((0,), (0,)), ((), ()))


def mm(left, right, dims=NN):
    return lax.dot_general(left, right, dims, preferred_element_type=f32)


def mm_exact(left, right, dims=NN):
    return lax.dot_general(left, right, dims, precision=highest, preferred_element_type=f32)


def low_lanes(shape):
    return lax.broadcasted_iota(jnp.int32, shape, 1) < P_SIZE


def softplus(values):
    return jnp.maximum(values, 0.0) + jnp.log1p(jnp.exp(-jnp.abs(values)))


def sigmoid(values):
    return 1.0 / (1.0 + jnp.exp(-values))


def at_or_after():
    rows = lax.broadcasted_iota(jnp.int32, (CHUNK, CHUNK), 0)
    columns = lax.broadcasted_iota(jnp.int32, (CHUNK, CHUNK), 1)
    return rows, columns


def convolved(ext_ref, taps_ref):
    taps = taps_ref.shape[0] - 1
    total = taps_ref[taps : taps + 1, :] + ext_ref[5 : 5 + CHUNK, :] * taps_ref[0:1, :]
    for k in range(1, taps):
        total = total + ext_ref[5 + k : 5 + k + CHUNK, :] * taps_ref[k : k + 1, :]
    return total


def pair_columns(table, pair):
    low = low_lanes((table.shape[0], LANES))
    return jnp.where(low, table[:, 2 * pair : 2 * pair + 1], table[:, 2 * pair + 1 : 2 * pair + 2])


def split_heads(values):
    low = low_lanes(values.shape)
    zero = jnp.zeros_like(values)
    return jnp.concatenate([jnp.where(low, values, zero), jnp.where(low, zero, values)], axis=0)


def mixer_forward_kernel(
    z_ref, u_ref, bc_ref, dr_ref, cx_ref, cbc_ref, hp_ref, g_ref, y_ref, h_ref, state, ext_u, ext_bc
):
    chunks = LEN // CHUNK
    first = lax.rem(pl.program_id(0), chunks) == 0
    pairs = u_ref.shape[1] // LANES
    states = bc_ref.shape[1] // 2

    @pl.when(first)
    def _():
        state[...] = jnp.zeros_like(state)
        ext_u[0:8, :] = jnp.zeros_like(ext_u[0:8, :])
        ext_bc[0:8, :] = jnp.zeros_like(ext_bc[0:8, :])

    @pl.when(jnp.logical_not(first))
    def _():
        ext_u[0:8, :] = ext_u[CHUNK : CHUNK + 8, :]
        ext_bc[0:8, :] = ext_bc[CHUNK : CHUNK + 8, :]

    ext_u[8 : 8 + CHUNK, :] = u_ref[...]
    ext_bc[8 : 8 + CHUNK, :] = bc_ref[...]
    v_x = convolved(ext_u, cx_ref)
    x = v_x * sigmoid(v_x)
    v_bc = convolved(ext_bc, cbc_ref)
    sc = (v_bc * sigmoid(v_bc)).astype(bf16)
    b_low, c_low = sc[:, :states], sc[:, states:]
    step = softplus(dr_ref[...] + hp_ref[0:1, :])
    decay = -step * jnp.exp(hp_ref[1:2, :])
    rows, columns = at_or_after()
    causal = rows >= columns
    cum = mm_exact(causal.astype(f32), decay)
    cum_t = cum.T
    inner = mm(c_low, b_low, NT)
    held = state[...]
    held_low = held.astype(bf16)
    h_ref[...] = held_low
    carried = mm(c_low, held_low)
    z = z_ref[...]
    gate = z * sigmoid(z)
    fresh = []
    for pair in range(pairs):
        at = slice(pair * LANES, (pair + 1) * LANES)
        x_pair = x[:, at]
        cum_pair = pair_columns(cum, pair)
        last = cum_pair[CHUNK - 1 : CHUNK, :]
        x_step = x_pair * pair_columns(step, pair)
        mixing = []
        for head in (2 * pair, 2 * pair + 1):
            spread = cum[:, head : head + 1] - cum_t[head : head + 1, :]
            mixing.append((jnp.exp(jnp.where(causal, spread, masked_score)) * inner).astype(bf16))
        out = mm(jnp.concatenate(mixing, axis=1), split_heads(x_step.astype(bf16)))
        out = out + carried[:, at] * jnp.exp(cum_pair)
        out = out + pair_columns(hp_ref[2:3, :], pair) * x_pair
        y_ref[:, at] = out.astype(bf16)
        g_ref[:, at] = (out * gate[:, at]).astype(bf16)
        fresh.append((x_step * jnp.exp(last - cum_pair)).astype(bf16))
        held_scale = jnp.exp(last)
        state[:, at] = held[:, at] * held_scale
    state[...] += mm(b_low, jnp.concatenate(fresh, axis=1), TN)


def mixer_backward_kernel(
    z_ref,
    u_ref,
    bc_ref,
    dr_ref,
    u_before_ref,
    bc_before_ref,
    y_ref,
    dg_ref,
    h_ref,
    att_ref,
    cx_ref,
    cbc_ref,
    hp_ref,
    hpt_ref,
    dproj_ref,
    wide_ref,
    bc_acc_ref,
    head_ref,
    state,
    ext_u,
    ext_bc,
    after_u,
    after_bc,
    da_rows,
):
    chunks = LEN // CHUNK
    step_id = pl.program_id(0)
    within = lax.rem(step_id, chunks)
    inner_cols = u_ref.shape[1]
    bc_cols = bc_ref.shape[1]
    pairs = inner_cols // LANES
    states = bc_cols // 2
    taps = cx_ref.shape[0] - 1

    @pl.when(step_id == 0)
    def _():
        wide_ref[...] = jnp.zeros_like(wide_ref)
        bc_acc_ref[...] = jnp.zeros_like(bc_acc_ref)
        head_ref[...] = jnp.zeros_like(head_ref)
        da_rows[...] = jnp.zeros_like(da_rows)

    @pl.when(within == 0)
    def _():
        state[...] = jnp.zeros_like(state)
        after_u[CHUNK:, :] = jnp.zeros_like(after_u[CHUNK:, :])
        after_bc[CHUNK:, :] = jnp.zeros_like(after_bc[CHUNK:, :])

    @pl.when(within > 0)
    def _():
        after_u[CHUNK:, :] = after_u[0:8, :]
        after_bc[CHUNK:, :] = after_bc[0:8, :]

    is_start = within == chunks - 1
    ext_u[0:8, :] = jnp.where(is_start, 0.0, u_before_ref[...])
    ext_bc[0:8, :] = jnp.where(is_start, 0.0, bc_before_ref[...])
    ext_u[8 : 8 + CHUNK, :] = u_ref[...]
    ext_bc[8 : 8 + CHUNK, :] = bc_ref[...]
    v_x = convolved(ext_u, cx_ref)
    sig_x = sigmoid(v_x)
    x = v_x * sig_x
    v_bc = convolved(ext_bc, cbc_ref)
    sig_bc = sigmoid(v_bc)
    sc = (v_bc * sig_bc).astype(bf16)
    b_low, c_low = sc[:, :states], sc[:, states:]
    raw = dr_ref[...]
    step = softplus(raw + hp_ref[0:1, :])
    decay = -step * jnp.exp(hp_ref[1:2, :])
    rows, columns = at_or_after()
    causal = rows >= columns
    cum = mm_exact(causal.astype(f32), decay)
    cum_t = cum.T
    inner_t = mm(b_low, c_low, NT)
    held_low = h_ref[...]
    carried = mm(c_low, held_low)
    next_grad = state[...]
    next_low = next_grad.astype(bf16)
    from_next = mm(b_low, next_low)
    z = z_ref[...]
    sig_z = sigmoid(z)
    gate = z * sig_z
    dg = dg_ref[...].astype(f32)
    dproj_ref[:, 0:inner_cols] = (
        dg * y_ref[...].astype(f32) * (sig_z * (1.0 + z * (1.0 - sig_z)))
    ).astype(bf16)
    dy = dg * gate
    later = rows <= columns
    reaches = causal.astype(bf16)
    inner_grad = jnp.zeros((CHUNK, CHUNK), f32)
    carry_terms, tail_terms, step_terms, dye_parts, xw_parts, held_terms = [], [], [], [], [], []
    for pair in range(pairs):
        at = slice(pair * LANES, (pair + 1) * LANES)
        x_pair = x[:, at]
        dy_pair = dy[:, at]
        cum_pair = pair_columns(cum, pair)
        last = cum_pair[CHUNK - 1 : CHUNK, :]
        step_pair = pair_columns(step, pair)
        x_step = x_pair * step_pair
        dy_low = dy_pair.astype(bf16)
        both = mm(split_heads(x_step.astype(bf16)), dy_low, NT)
        mixing, products = [], []
        for part, head in enumerate((2 * pair, 2 * pair + 1)):
            spread = cum_t[head : head + 1, :] - cum[:, head : head + 1]
            decayed = jnp.exp(jnp.where(later, spread, masked_score))
            grad_part = decayed * both[part * CHUNK : (part + 1) * CHUNK, :]
            inner_grad = inner_grad + grad_part
            products.append((grad_part * inner_t).astype(bf16))
            mixing.append((decayed * inner_t).astype(bf16))
        reach = mm(jnp.concatenate(products, axis=0), reaches)
        for part, head in enumerate((2 * pair, 2 * pair + 1)):
            block = reach[part * CHUNK : (part + 1) * CHUNK, :]
            da_rows[head : head + 1, :] = jnp.sum(
                jnp.where(rows < columns, block, 0.0), axis=0, keepdims=True
            )
        x_grad = mm(jnp.concatenate(mixing, axis=1), split_heads(dy_low))
        grown = jnp.exp(cum_pair)
        dye = dy_pair * grown
        dye_low = dye.astype(bf16)
        dye_parts.append(dye_low)
        carry_terms.append((dye * carried[:, at]).astype(bf16))
        tail = jnp.exp(last - cum_pair)
        x_tail = tail * from_next[:, at]
        tail_terms.append((x_step * x_tail).astype(bf16))
        xw_parts.append((x_step * tail).astype(bf16))
        x_grad = x_grad + x_tail
        step_terms.append((x_pair * x_grad).astype(bf16))
        skip_gain = pair_columns(hp_ref[2:3, :], pair)
        uc_grad = step_pair * x_grad + skip_gain * dy_pair
        v_pair, s_pair = v_x[:, at], sig_x[:, at]
        after_u[0:CHUNK, at] = uc_grad * (s_pair * (1.0 + v_pair * (1.0 - s_pair)))
        wide_ref[taps + 1 : taps + 2, at] += jnp.sum(dy_pair * x_pair, axis=0, keepdims=True)
        held_scale = jnp.exp(last)
        kept = next_grad[:, at] * held_scale
        held_terms.append(jnp.sum(kept * held_low[:, at].astype(f32), axis=0, keepdims=True))
        state[:, at] = kept
    dye_all = jnp.concatenate(dye_parts, axis=1)
    xw_all = jnp.concatenate(xw_parts, axis=1)
    state[...] += mm(c_low, dye_all, TN)
    inner_grad_low = inner_grad.astype(bf16)
    b_grad = mm(inner_grad_low, c_low) + mm(xw_all, next_low, NT)
    c_grad = mm(inner_grad_low, b_low, TN) + mm(dye_all, held_low, NT)
    sc_grad = jnp.concatenate([b_grad, c_grad], axis=1)
    after_bc[0:CHUNK, :] = sc_grad * (sig_bc * (1.0 + v_bc * (1.0 - sig_bc)))

    head_ids = lax.broadcasted_iota(jnp.int32, (HEAD_ROWS, inner_cols), 0)
    channels = lax.broadcasted_iota(jnp.int32, (HEAD_ROWS, inner_cols), 1)
    members = (lax.div(channels, P_SIZE) == head_ids).astype(bf16)
    carry_row = mm(members, jnp.concatenate(carry_terms, axis=1), NT)
    tail_row = mm(members, jnp.concatenate(tail_terms, axis=1), NT)
    step_row = mm(members, jnp.concatenate(step_terms, axis=1), NT)
    held_row = jnp.concatenate(held_terms, axis=1)
    held_col = jnp.sum(
        jnp.where(lax.div(channels, P_SIZE) == head_ids, held_row, 0.0), axis=1, keepdims=True
    )
    decay_grad = (
        da_rows[...]
        + mm_exact(carry_row, causal.astype(f32))
        + mm_exact(tail_row, (rows < columns).astype(f32))
        + held_col
    )
    raw_t = raw.T[:HEAD_ROWS, :] + hpt_ref[:, 0:1]
    step_t = softplus(raw_t)
    rate = -jnp.exp(hpt_ref[:, 1:2])
    step_grad = step_row + decay_grad * rate
    real = lax.broadcasted_iota(jnp.int32, (HEAD_ROWS, CHUNK), 0) < 2 * pairs
    raw_grad = jnp.where(real, step_grad * sigmoid(raw_t), 0.0)
    head_ref[0:HEAD_ROWS, :] += raw_grad
    head_ref[HEAD_ROWS:, :] += jnp.where(real, decay_grad * rate * step_t, 0.0)
    raw_grad_cols = jnp.concatenate(
        [raw_grad, jnp.zeros((LANES - HEAD_ROWS, CHUNK), f32)], axis=0
    ).T

    base = 2 * inner_cols
    for ext_ref, after_ref, taps_ref, acc_ref, start in (
        (ext_u, after_u, cx_ref, wide_ref, inner_cols),
        (ext_bc, after_bc, cbc_ref, bc_acc_ref, base),
    ):
        width = after_ref.shape[1]
        conv_grad = after_ref[0:CHUNK, :]
        value_grad = after_ref[taps - 1 : taps - 1 + CHUNK, :] * taps_ref[0:1, :]
        for k in range(1, taps):
            shift = taps - 1 - k
            value_grad = value_grad + after_ref[shift : shift + CHUNK, :] * taps_ref[k : k + 1, :]
        dproj_ref[:, start : start + width] = value_grad.astype(bf16)
        for k in range(taps):
            acc_ref[k : k + 1, :] += jnp.sum(
                conv_grad * ext_ref[5 + k : 5 + k + CHUNK, :], axis=0, keepdims=True
            )
        acc_ref[taps : taps + 1, :] += jnp.sum(conv_grad, axis=0, keepdims=True)
    att_cols = att_ref.shape[1]
    dproj_ref[:, base + bc_cols : base + bc_cols + att_cols] = att_ref[...]
    dproj_ref[:, base + bc_cols + att_cols :] = raw_grad_cols.astype(bf16)


def swap_halves(values):
    half = P_SIZE // 2
    lane = lax.broadcasted_iota(jnp.int32, values.shape, 1)
    first = lax.rem(lane, P_SIZE) < half
    return jnp.where(
        first, pltpu.roll(values, LANES - half, axis=1), pltpu.roll(values, half, axis=1)
    )


def rotated(values, cosine, sine):
    return values * cosine + swap_halves(values) * sine


def rotated_back(values, cosine, sine):
    return values * cosine - swap_halves(values) * sine


def keys_and_values(kv_ref, cos_ref, sin_ref):
    kv = kv_ref[...]
    low = low_lanes(kv.shape)
    turned = rotated(kv, cos_ref[...], sin_ref[...])
    keys = jnp.where(low, turned, pltpu.roll(turned, P_SIZE, axis=1)).astype(bf16)
    values = jnp.where(low, pltpu.roll(kv, P_SIZE, axis=1), kv).astype(bf16)
    return keys, values


def score_weights(queries, keys, start):
    scores = mm(queries, keys, NT)
    rows = lax.broadcasted_iota(jnp.int32, scores.shape, 0) + start
    columns = lax.broadcasted_iota(jnp.int32, scores.shape, 1)
    scores = jnp.where(rows >= columns, scores, masked_score)
    weights = jnp.exp(scores - jnp.max(scores, axis=1, keepdims=True))
    return weights * (1.0 / jnp.sum(weights, axis=1, keepdims=True))


def rotated_queries(q_ref, cos_ref, sin_ref, here, at):
    turned = rotated(q_ref[here, at], cos_ref[here, :], sin_ref[here, :]).astype(bf16)
    return turned * jnp.asarray(P_SIZE**-0.5, bf16)


def attention_forward_kernel(q_ref, kv_ref, cos_ref, sin_ref, o_ref):
    keys, values = keys_and_values(kv_ref, cos_ref, sin_ref)
    for block in range(LEN // QBLOCK):
        here = slice(block * QBLOCK, (block + 1) * QBLOCK)
        seen = (block + 1) * QBLOCK
        for pair in range(q_ref.shape[1] // LANES):
            at = slice(pair * LANES, (pair + 1) * LANES)
            queries = rotated_queries(q_ref, cos_ref, sin_ref, here, at)
            low = low_lanes(queries.shape)
            zero = jnp.zeros_like(queries)
            outs = []
            for chosen in (jnp.where(low, queries, zero), jnp.where(low, zero, queries)):
                weights = score_weights(chosen, keys[:seen], block * QBLOCK)
                outs.append(mm(weights.astype(bf16), values[:seen]))
            o_ref[here, at] = jnp.where(low_lanes(outs[0].shape), outs[0], outs[1]).astype(bf16)


def attention_backward_kernel(
    q_ref, kv_ref, cos_ref, sin_ref, do_ref, grad_ref, key_grad, value_grad
):
    keys, values = keys_and_values(kv_ref, cos_ref, sin_ref)
    key_grad[...] = jnp.zeros_like(key_grad)
    value_grad[...] = jnp.zeros_like(value_grad)
    q_cols = q_ref.shape[1]
    for block in range(LEN // QBLOCK):
        here = slice(block * QBLOCK, (block + 1) * QBLOCK)
        seen = (block + 1) * QBLOCK
        for pair in range(q_cols // LANES):
            at = slice(pair * LANES, (pair + 1) * LANES)
            queries = rotated_queries(q_ref, cos_ref, sin_ref, here, at)
            out_grad = do_ref[here, at].astype(bf16)
            low = low_lanes(queries.shape)
            zero = jnp.zeros_like(queries)
            parts = []
            for is_low in (True, False):
                q_one = jnp.where(low, queries, zero) if is_low else jnp.where(low, zero, queries)
                g_one = jnp.where(low, out_grad, zero) if is_low else jnp.where(low, zero, out_grad)
                weights = score_weights(q_one, keys[:seen], block * QBLOCK)
                weight_grad = mm(g_one, values[:seen], NT)
                inner = jnp.sum(weights * weight_grad, axis=1, keepdims=True)
                score_grad = (weights * (weight_grad - inner)).astype(bf16)
                parts.append(mm(score_grad, keys[:seen]))
                key_grad[:seen, :] += mm(score_grad, q_one, TN)
                value_grad[:seen, :] += mm(weights.astype(bf16), g_one, TN)
            turned = jnp.where(low_lanes(parts[0].shape), parts[0], parts[1]) * P_SIZE**-0.5
            grad_ref[here, at] = rotated_back(turned, cos_ref[here, :], sin_ref[here, :]).astype(
                bf16
            )
    keys_sum = key_grad[...]
    keys_sum = keys_sum + pltpu.roll(keys_sum, P_SIZE, axis=1)
    values_sum = value_grad[...]
    values_sum = values_sum + pltpu.roll(values_sum, P_SIZE, axis=1)
    keys_sum = rotated_back(keys_sum, cos_ref[...], sin_ref[...])
    grad_ref[:, q_cols:] = jnp.where(low_lanes(keys_sum.shape), keys_sum, values_sum).astype(bf16)


def rotary_tables():
    half = P_SIZE // 2
    frequency = jnp.exp(jnp.arange(half, dtype=f32) * (-2.0 * math.log(rope_base) / P_SIZE))
    angles = jnp.arange(LEN, dtype=f32)[:, None] * frequency[None, :]
    cosine, sine = jnp.cos(angles), jnp.sin(angles)
    return (
        jnp.concatenate([cosine, cosine, cosine, cosine], axis=1),
        jnp.concatenate([-sine, sine, -sine, sine], axis=1),
    )


def vmem_params(megabytes):
    return pltpu.CompilerParams(
        vmem_limit_bytes=megabytes * 1024 * 1024, dimension_semantics=("arbitrary",)
    )


def mixer_forward(proj, conv_x, conv_bc, heads, inner_cols, bc_cols):
    rows_all = proj.shape[0]
    states = bc_cols // 2
    bc_at = 2 * inner_cols // bc_cols
    dt_at = proj.shape[1] // LANES - 1
    steps = rows_all // CHUNK
    return pl.pallas_call(
        mixer_forward_kernel,
        grid=(steps,),
        in_specs=[
            pl.BlockSpec((CHUNK, inner_cols), lambda i: (i, 0)),
            pl.BlockSpec((CHUNK, inner_cols), lambda i: (i, 1)),
            pl.BlockSpec((CHUNK, bc_cols), lambda i: (i, bc_at)),
            pl.BlockSpec((CHUNK, LANES), lambda i: (i, dt_at)),
            pl.BlockSpec(conv_x.shape, lambda i: (0, 0)),
            pl.BlockSpec(conv_bc.shape, lambda i: (0, 0)),
            pl.BlockSpec(heads.shape, lambda i: (0, 0)),
        ],
        out_specs=[
            pl.BlockSpec((CHUNK, inner_cols), lambda i: (i, 0)),
            pl.BlockSpec((CHUNK, inner_cols), lambda i: (i, 0)),
            pl.BlockSpec((states, inner_cols), lambda i: (i, 0)),
        ],
        out_shape=[
            jax.ShapeDtypeStruct((rows_all, inner_cols), bf16),
            jax.ShapeDtypeStruct((rows_all, inner_cols), bf16),
            jax.ShapeDtypeStruct((steps * states, inner_cols), bf16),
        ],
        scratch_shapes=[
            pltpu.VMEM((states, inner_cols), f32),
            pltpu.VMEM((CHUNK + 8, inner_cols), f32),
            pltpu.VMEM((CHUNK + 8, bc_cols), f32),
        ],
        compiler_params=vmem_params(32),
        cost_estimate=pl.CostEstimate(
            flops=rows_all * inner_cols * 1200,
            bytes_accessed=rows_all * inner_cols * 14,
            transcendentals=rows_all * inner_cols * 4,
        ),
        name="mixer_forward",
    )(proj, proj, proj, proj, conv_x, conv_bc, heads)


def mixer_backward(proj, y, dg, held, att_grad, conv_x, conv_bc, heads, inner_cols, bc_cols):
    rows_all = proj.shape[0]
    states = bc_cols // 2
    bc_at = 2 * inner_cols // bc_cols
    dt_at = proj.shape[1] // LANES - 1
    steps = rows_all // CHUNK
    chunks = LEN // CHUNK
    per = CHUNK // 8

    def at(i):
        return i // chunks * chunks + (chunks - 1 - i % chunks)

    def before(i):
        return jnp.maximum(at(i) * per - 1, 0)

    heads_t = heads[:, :HEAD_ROWS].T
    return pl.pallas_call(
        mixer_backward_kernel,
        grid=(steps,),
        in_specs=[
            pl.BlockSpec((CHUNK, inner_cols), lambda i: (at(i), 0)),
            pl.BlockSpec((CHUNK, inner_cols), lambda i: (at(i), 1)),
            pl.BlockSpec((CHUNK, bc_cols), lambda i: (at(i), bc_at)),
            pl.BlockSpec((CHUNK, LANES), lambda i: (at(i), dt_at)),
            pl.BlockSpec((8, inner_cols), lambda i: (before(i), 1)),
            pl.BlockSpec((8, bc_cols), lambda i: (before(i), bc_at)),
            pl.BlockSpec((CHUNK, inner_cols), lambda i: (at(i), 0)),
            pl.BlockSpec((CHUNK, inner_cols), lambda i: (at(i), 0)),
            pl.BlockSpec((states, inner_cols), lambda i: (at(i), 0)),
            pl.BlockSpec((CHUNK, att_grad.shape[1]), lambda i: (at(i), 0)),
            pl.BlockSpec(conv_x.shape, lambda i: (0, 0)),
            pl.BlockSpec(conv_bc.shape, lambda i: (0, 0)),
            pl.BlockSpec(heads.shape, lambda i: (0, 0)),
            pl.BlockSpec(heads_t.shape, lambda i: (0, 0)),
        ],
        out_specs=[
            pl.BlockSpec((CHUNK, proj.shape[1]), lambda i: (at(i), 0)),
            pl.BlockSpec((8, inner_cols), lambda i: (0, 0)),
            pl.BlockSpec((8, bc_cols), lambda i: (0, 0)),
            pl.BlockSpec((2 * HEAD_ROWS, CHUNK), lambda i: (0, 0)),
        ],
        out_shape=[
            jax.ShapeDtypeStruct(proj.shape, bf16),
            jax.ShapeDtypeStruct((8, inner_cols), f32),
            jax.ShapeDtypeStruct((8, bc_cols), f32),
            jax.ShapeDtypeStruct((2 * HEAD_ROWS, CHUNK), f32),
        ],
        scratch_shapes=[
            pltpu.VMEM((states, inner_cols), f32),
            pltpu.VMEM((CHUNK + 8, inner_cols), f32),
            pltpu.VMEM((CHUNK + 8, bc_cols), f32),
            pltpu.VMEM((CHUNK + 8, inner_cols), f32),
            pltpu.VMEM((CHUNK + 8, bc_cols), f32),
            pltpu.VMEM((HEAD_ROWS, CHUNK), f32),
        ],
        compiler_params=vmem_params(48),
        cost_estimate=pl.CostEstimate(
            flops=rows_all * inner_cols * 4000,
            bytes_accessed=rows_all * inner_cols * 26,
            transcendentals=rows_all * inner_cols * 8,
        ),
        name="mixer_backward",
    )(
        proj, proj, proj, proj, proj, proj, y, dg, held, att_grad, conv_x, conv_bc, heads, heads_t
    )


def attention_forward(proj, tables, q_cols, q_at, kv_at):
    rows_all = proj.shape[0]
    return pl.pallas_call(
        attention_forward_kernel,
        grid=(rows_all // LEN,),
        in_specs=[
            pl.BlockSpec((LEN, q_cols), lambda i: (i, q_at)),
            pl.BlockSpec((LEN, LANES), lambda i: (i, kv_at)),
            pl.BlockSpec((LEN, LANES), lambda i: (0, 0)),
            pl.BlockSpec((LEN, LANES), lambda i: (0, 0)),
        ],
        out_specs=pl.BlockSpec((LEN, q_cols), lambda i: (i, 0)),
        out_shape=jax.ShapeDtypeStruct((rows_all, q_cols), bf16),
        compiler_params=vmem_params(40),
        cost_estimate=pl.CostEstimate(
            flops=rows_all * LEN * q_cols * 8,
            bytes_accessed=rows_all * q_cols * 12,
            transcendentals=rows_all * LEN * 3,
        ),
        name="attention_forward",
    )(proj, proj, *tables)


def attention_backward(proj, tables, out_grad, q_cols, q_at, kv_at):
    rows_all = proj.shape[0]
    return pl.pallas_call(
        attention_backward_kernel,
        grid=(rows_all // LEN,),
        in_specs=[
            pl.BlockSpec((LEN, q_cols), lambda i: (i, q_at)),
            pl.BlockSpec((LEN, LANES), lambda i: (i, kv_at)),
            pl.BlockSpec((LEN, LANES), lambda i: (0, 0)),
            pl.BlockSpec((LEN, LANES), lambda i: (0, 0)),
            pl.BlockSpec((LEN, q_cols), lambda i: (i, out_grad.shape[1] // q_cols - 1)),
        ],
        out_specs=pl.BlockSpec((LEN, q_cols + LANES), lambda i: (i, 0)),
        out_shape=jax.ShapeDtypeStruct((rows_all, q_cols + LANES), bf16),
        scratch_shapes=[pltpu.VMEM((LEN, LANES), f32), pltpu.VMEM((LEN, LANES), f32)],
        compiler_params=vmem_params(48),
        cost_estimate=pl.CostEstimate(
            flops=rows_all * LEN * q_cols * 20,
            bytes_accessed=rows_all * q_cols * 16,
            transcendentals=rows_all * LEN * 3,
        ),
        name="attention_backward",
    )(proj, proj, *tables, out_grad)


def inverse_rms(values):
    return lax.rsqrt(jnp.mean(values * values, axis=-1, keepdims=True) + epsilon)


def normalize_back(grad, values, inverse, gain_row):
    unit = values * inverse
    scaled = grad * gain_row
    return (scaled - unit * jnp.mean(scaled * unit, axis=-1, keepdims=True)) * inverse


def swap_tensor(values):
    return lax.ppermute(values, "tensor", [(0, 1), (1, 0)])


def both_halves(mine):
    other = swap_tensor(mine)
    return jnp.where(
        lax.axis_index("tensor") == 0,
        jnp.concatenate([mine, other], axis=0),
        jnp.concatenate([other, mine], axis=0),
    )


def half_rows(values, index):
    rows = values.shape[0] // 2
    return lax.dynamic_slice_in_dim(values, index * rows, rows, 0)


def sum_own_half(values, index):
    arrived = swap_tensor(half_rows(values, 1 - index))
    return half_rows(values, index).astype(f32) + arrived.astype(f32)


def scatter_sum(values, dp_count):
    pairs = dp_count // 2
    core = lax.rem(lax.axis_index("dp"), 2)
    by_core = values.reshape(pairs, 2, values.shape[0] // dp_count, values.shape[1])
    kept = lax.dynamic_index_in_dim(by_core, core, 1, keepdims=False)
    sent = lax.dynamic_index_in_dim(by_core, 1 - core, 1, keepdims=False)
    arrived = lax.ppermute(sent, "dp", [(i, i ^ 1) for i in range(dp_count)])
    summed = (kept.astype(f32) + arrived.astype(f32)).astype(bf16)
    groups = [[core_id + 2 * i for i in range(pairs)] for core_id in range(2)]
    blocks = lax.all_to_all(summed, "dp", 0, 0, tiled=True, axis_index_groups=groups)
    return jnp.sum(blocks.astype(f32), axis=0)


def local(
    tokens,
    gains,
    w_zx,
    w_bc,
    w_dt,
    conv_x,
    conv_bc,
    head_params,
    w_mo,
    w_q,
    w_kv,
    w_ao,
    w_gu,
    w_down,
    cotangent,
):
    dp_count = lax.axis_size("dp")
    side = lax.axis_index("tensor")
    width = tokens.shape[1]
    here = width // dp_count
    inner_cols, bc_cols, head_cols = w_zx.shape[2], w_bc.shape[1], w_dt.shape[1]
    q_cols, kv_cols = w_q.shape[1], 2 * w_kv.shape[2]
    hidden, mo_cols, ao_cols = w_gu.shape[2], w_mo.shape[0], w_ao.shape[0]

    shared = both_halves(jnp.concatenate([w_bc, gains.T], axis=1))
    in_pack = jnp.concatenate(
        [
            w_zx[:, 0],
            w_zx[:, 1],
            shared[:, :bc_cols],
            w_q,
            w_kv.reshape(here, kv_cols),
            w_dt,
            shared[:, bc_cols:],
            jnp.zeros((here, LANES - head_cols - 2), bf16),
        ],
        axis=1,
    )
    w_in = lax.all_gather(in_pack, "dp", axis=0, tiled=True)
    out_pack = jnp.concatenate(
        [w_gu.reshape(here, 2 * hidden), w_down.T, w_mo.T, w_ao.T], axis=1
    )
    w_out = lax.all_gather(out_pack, "dp", axis=0, tiled=True)
    tokens_all = both_halves(tokens)
    cotangent_all = both_halves(cotangent)
    tables = rotary_tables()

    gu_full = w_out[:, : 2 * hidden]
    down_full = w_out[:, 2 * hidden : 3 * hidden]
    mix_full = w_out[:, 3 * hidden :]
    dt_start = w_in.shape[1] - LANES
    gain_full = w_in[:, dt_start + head_cols : dt_start + head_cols + 2].T.astype(f32)
    gain_one, gain_two = gain_full[0:1], gain_full[1:2]
    heads = jnp.pad(head_params, ((0, 5), (0, LANES - head_cols)))
    q_at = (2 * inner_cols + bc_cols) // q_cols
    kv_at = (2 * inner_cols + bc_cols + q_cols) // LANES

    seq_in = tokens_all.astype(f32)
    inverse_one = inverse_rms(seq_in)
    n1 = (seq_in * inverse_one * gain_one).astype(bf16)
    proj = mm(n1, w_in)
    gated, y, held = mixer_forward(proj, conv_x, conv_bc, heads, inner_cols, bc_cols)
    attended = attention_forward(proj, tables, q_cols, q_at, kv_at)
    branch_part = mm(gated, mix_full[:, :mo_cols], NT) + mm(attended, mix_full[:, mo_cols:], NT)
    branch_low = branch_part.astype(bf16)
    branch = branch_low.astype(f32) + swap_tensor(branch_low).astype(f32)
    hidden_one = seq_in + branch
    inverse_two = inverse_rms(hidden_one)
    n2 = (hidden_one * inverse_two * gain_two).astype(bf16)
    gate_up = mm(n2, gu_full)
    gate, up = gate_up[:, :hidden], gate_up[:, hidden:]
    sig = sigmoid(gate)
    activated = (gate * sig * up).astype(bf16)
    ffn_low = mm(activated, down_full, NT).astype(bf16)
    layer_out = (half_rows(hidden_one, side) + sum_own_half(ffn_low, side)).astype(bf16)

    act_grad = mm(cotangent_all, down_full)
    gate_up_grad = jnp.concatenate(
        [act_grad * up * (sig * (1.0 + gate * (1.0 - sig))), act_grad * (gate * sig)], axis=1
    ).astype(bf16)
    n2_grad_low = mm(gate_up_grad, gu_full, NT).astype(bf16)
    ffn_grads = jnp.concatenate(
        [
            mm(n2, gate_up_grad, TN).astype(bf16),
            mm(cotangent_all, activated, TN).astype(bf16),
        ],
        axis=1,
    )
    ffn_grads = lax.psum_scatter(ffn_grads, "dp", scatter_dimension=0, tiled=True)
    n2_grad = n2_grad_low.astype(f32) + swap_tensor(n2_grad_low).astype(f32)
    gain_two_grad = jnp.sum(n2_grad_low.astype(f32) * (hidden_one * inverse_two), axis=0)
    hidden_grad = cotangent_all.astype(f32) + normalize_back(
        n2_grad, hidden_one, inverse_two, gain_two
    )
    branch_grad = hidden_grad.astype(bf16)
    mix_grad = mm(branch_grad, mix_full).astype(bf16)
    mo_grad = mm(branch_grad, gated, TN).astype(bf16)
    ao_grad = mm(branch_grad, attended, TN).astype(bf16)
    att_grad = attention_backward(proj, tables, mix_grad, q_cols, q_at, kv_at)
    proj_grad, wide_sums, bc_sums, head_sums = mixer_backward(
        proj, y, mix_grad, held, att_grad, conv_x, conv_bc, heads, inner_cols, bc_cols
    )
    n1_grad_low = mm(proj_grad, w_in, NT).astype(bf16)
    gain_one_grad = jnp.sum(n1_grad_low.astype(f32) * (seq_in * inverse_one), axis=0)
    in_grads = mm(n1, proj_grad, TN).astype(bf16)
    n1_grad = sum_own_half(n1_grad_low, side)
    seq_own = tokens.astype(f32)
    input_grad = (
        half_rows(hidden_grad, side)
        + normalize_back(n1_grad, seq_own, inverse_rms(seq_own), gain_one)
    ).astype(bf16)

    taps = conv_x.shape[0]
    head_grads = jnp.stack(
        [
            jnp.sum(head_sums[:head_cols], axis=1),
            jnp.sum(head_sums[HEAD_ROWS : HEAD_ROWS + head_cols], axis=1),
            jnp.sum(wide_sums[taps].reshape(head_cols, P_SIZE), axis=1),
        ]
    )
    pieces = [wide_sums[:taps], bc_sums[:taps], head_grads]
    flat = jnp.concatenate([piece.reshape(-1) for piece in pieces])
    flat_cols = -(-flat.shape[0] // here)
    flat_cols = -(-(flat_cols + 2) // LANES) * LANES - 2
    flat = jnp.pad(flat, (0, here * flat_cols - flat.shape[0])).reshape(here, flat_cols)
    gain_cols = jnp.stack([gain_one_grad, gain_two_grad], axis=1)
    small = jnp.concatenate([gain_cols, jnp.tile(flat, (dp_count, 1))], axis=1).astype(bf16)
    summed = scatter_sum(
        jnp.concatenate([in_grads, mo_grad, ao_grad, small], axis=1), dp_count
    )

    in_cols = in_grads.shape[1]
    bc_start = 2 * inner_cols
    q_start = bc_start + bc_cols
    kv_start = q_start + q_cols
    mo_start = in_cols
    ao_start = mo_start + mo_cols
    gain_start = ao_start + ao_cols
    flat_sum = summed[:, gain_start + 2 :].reshape(-1)
    x_size, bc_size = taps * inner_cols, taps * bc_cols
    grad_conv_x = flat_sum[:x_size].reshape(taps, inner_cols)
    conv_bc_half = flat_sum[x_size : x_size + bc_size].reshape(taps, bc_cols)
    grad_head = flat_sum[x_size + bc_size : x_size + bc_size + 3 * head_cols].reshape(3, head_cols)
    shared_half = jnp.concatenate(
        [summed[:, bc_start:q_start], summed[:, gain_start : gain_start + 2]], axis=1
    )
    to_send = jnp.concatenate(
        [half_rows(shared_half, 1 - side).reshape(-1), conv_bc_half.reshape(-1)]
    )
    arrived = swap_tensor(to_send)
    shared_sum = half_rows(shared_half, side) + arrived[: shared_half.size // 2].reshape(
        here // 2, bc_cols + 2
    )
    grad_conv_bc = conv_bc_half + arrived[shared_half.size // 2 :].reshape(taps, bc_cols)
    ffn_sum = ffn_grads.astype(f32)
    return (
        layer_out,
        input_grad,
        shared_sum[:, bc_cols:].T,
        summed[:, :bc_start].reshape(here, 2, inner_cols),
        shared_sum[:, :bc_cols],
        summed[:, dt_start : dt_start + head_cols],
        grad_conv_x,
        grad_conv_bc,
        grad_head,
        summed[:, mo_start:ao_start].T,
        summed[:, q_start:kv_start],
        summed[:, kv_start : kv_start + kv_cols].reshape(here, 2, kv_cols // 2),
        summed[:, ao_start:gain_start].T,
        ffn_sum[:, : 2 * hidden].reshape(here, 2, hidden),
        ffn_sum[:, 2 * hidden :].T,
    )


def solution(mesh):
    placed = (
        P(("dp", "tensor"), None),
        P(None, ("dp", "tensor")),
        P("dp", None, "tensor"),
        P(("dp", "tensor"), None),
        P("dp", "tensor"),
        P(None, "tensor"),
        P(),
        P(None, "tensor"),
        P("tensor", "dp"),
        P("dp", "tensor"),
        P("dp", None, "tensor"),
        P("tensor", "dp"),
        P("dp", None, "tensor"),
        P("tensor", "dp"),
        P(("dp", "tensor"), None),
    )
    return jax.shard_map(
        local,
        mesh=mesh,
        in_specs=placed,
        out_specs=(
            P(("dp", "tensor"), None),
            P(("dp", "tensor"), None),
            P(None, ("dp", "tensor")),
            P("dp", None, "tensor"),
            P(("dp", "tensor"), None),
            P("dp", "tensor"),
            P(None, "tensor"),
            P(),
            P(None, "tensor"),
            P("tensor", "dp"),
            P("dp", "tensor"),
            P("dp", None, "tensor"),
            P("tensor", "dp"),
            P("dp", None, "tensor"),
            P("tensor", "dp"),
        ),
        check_vma=False,
    )
```

```python
import functools
import math

import jax
import jax.numpy as jnp
from jax import lax
from jax.experimental import pallas as pl
from jax.experimental.pallas import tpu as pltpu
from jax.sharding import PartitionSpec as P

P_SIZE = 64
LEN = 1024
CHUNK = 128
LANES = 128
QBLOCK = 256
HEAD_ROWS = 16
ROW_PARTS = 2
HIDDEN_BLOCK = 512

highest = lax.Precision.HIGHEST
epsilon = 1e-05
rope_base = 100000000000.0
masked_score = -1e30
f32 = jnp.float32
bf16 = jnp.bfloat16

NN = (((1,), (0,)), ((), ()))
NT = (((1,), (1,)), ((), ()))
TN = (((0,), (0,)), ((), ()))
TT = (((0,), (1,)), ((), ()))


def mm(left, right, dims=NN):
    return lax.dot_general(left, right, dims, preferred_element_type=f32)


def mm_exact(left, right, dims=NN):
    return lax.dot_general(left, right, dims, precision=highest, preferred_element_type=f32)


def low_lanes(shape):
    return lax.broadcasted_iota(jnp.int32, shape, 1) < P_SIZE


def softplus(values):
    return jnp.maximum(values, 0.0) + jnp.log1p(jnp.exp(-jnp.abs(values)))


def sigmoid(values):
    return 1.0 / (1.0 + jnp.exp(-values))


def at_or_after():
    rows = lax.broadcasted_iota(jnp.int32, (CHUNK, CHUNK), 0)
    columns = lax.broadcasted_iota(jnp.int32, (CHUNK, CHUNK), 1)
    return rows, columns


def convolved(ext_ref, taps_ref):
    taps = taps_ref.shape[0] - 1
    total = taps_ref[taps : taps + 1, :] + ext_ref[5 : 5 + CHUNK, :] * taps_ref[0:1, :]
    for k in range(1, taps):
        total = total + ext_ref[5 + k : 5 + k + CHUNK, :] * taps_ref[k : k + 1, :]
    return total


def pair_columns(table, pair):
    low = low_lanes((table.shape[0], LANES))
    return jnp.where(low, table[:, 2 * pair : 2 * pair + 1], table[:, 2 * pair + 1 : 2 * pair + 2])


def split_heads(values):
    low = low_lanes(values.shape)
    zero = jnp.zeros_like(values)
    return jnp.concatenate([jnp.where(low, values, zero), jnp.where(low, zero, values)], axis=0)


def mixer_forward_kernel(
    z_ref, u_ref, bc_ref, dr_ref, cx_ref, cbc_ref, hp_ref, g_ref, y_ref, h_ref, state, ext_u, ext_bc
):
    chunks = LEN // CHUNK
    first = lax.rem(pl.program_id(0), chunks) == 0
    pairs = u_ref.shape[1] // LANES
    states = bc_ref.shape[1] // 2

    @pl.when(first)
    def _():
        state[...] = jnp.zeros_like(state)
        ext_u[0:8, :] = jnp.zeros_like(ext_u[0:8, :])
        ext_bc[0:8, :] = jnp.zeros_like(ext_bc[0:8, :])

    @pl.when(jnp.logical_not(first))
    def _():
        ext_u[0:8, :] = ext_u[CHUNK : CHUNK + 8, :]
        ext_bc[0:8, :] = ext_bc[CHUNK : CHUNK + 8, :]

    ext_u[8 : 8 + CHUNK, :] = u_ref[...]
    ext_bc[8 : 8 + CHUNK, :] = bc_ref[...]
    v_x = convolved(ext_u, cx_ref)
    x = v_x * sigmoid(v_x)
    v_bc = convolved(ext_bc, cbc_ref)
    sc = (v_bc * sigmoid(v_bc)).astype(bf16)
    b_low, c_low = sc[:, :states], sc[:, states:]
    step = softplus(dr_ref[...] + hp_ref[0:1, :])
    decay = -step * jnp.exp(hp_ref[1:2, :])
    rows, columns = at_or_after()
    causal = rows >= columns
    cum = mm_exact(causal.astype(f32), decay)
    cum_t = cum.T
    inner = mm(c_low, b_low, NT)
    held = state[...]
    held_low = held.astype(bf16)
    h_ref[...] = held_low
    carried = mm(c_low, held_low)
    z = z_ref[...]
    gate = z * sigmoid(z)
    fresh = []
    for pair in range(pairs):
        at = slice(pair * LANES, (pair + 1) * LANES)
        x_pair = x[:, at]
        cum_pair = pair_columns(cum, pair)
        last = cum_pair[CHUNK - 1 : CHUNK, :]
        x_step = x_pair * pair_columns(step, pair)
        mixing = []
        for head in (2 * pair, 2 * pair + 1):
            spread = cum[:, head : head + 1] - cum_t[head : head + 1, :]
            mixing.append((jnp.exp(jnp.where(causal, spread, masked_score)) * inner).astype(bf16))
        out = mm(jnp.concatenate(mixing, axis=1), split_heads(x_step.astype(bf16)))
        out = out + carried[:, at] * jnp.exp(cum_pair)
        out = out + pair_columns(hp_ref[2:3, :], pair) * x_pair
        y_ref[:, at] = out.astype(bf16)
        g_ref[:, at] = (out * gate[:, at]).astype(bf16)
        fresh.append((x_step * jnp.exp(last - cum_pair)).astype(bf16))
        held_scale = jnp.exp(last)
        state[:, at] = held[:, at] * held_scale
    state[...] += mm(b_low, jnp.concatenate(fresh, axis=1), TN)


def mixer_backward_kernel(
    z_ref,
    u_ref,
    bc_ref,
    dr_ref,
    u_before_ref,
    bc_before_ref,
    y_ref,
    dg_ref,
    h_ref,
    cx_ref,
    cbc_ref,
    hp_ref,
    hpt_ref,
    carry_in_ref,
    *rest,
    is_start_part,
):
    dproj_ref, carry_ref, ext_u, ext_bc, after_u, after_bc, da_rows = rest[-7:]
    step_id = pl.program_id(0)
    inner_cols = u_ref.shape[1]
    bc_cols = bc_ref.shape[1]
    pairs = inner_cols // LANES
    states = bc_cols // 2
    taps = cx_ref.shape[0] - 1
    state = carry_ref.at[0:states, :]
    kept_u = carry_ref.at[states : states + 8, :]
    wide_ref = carry_ref.at[states + 8 : states + 16, :]
    kept_bc = carry_ref.at[states + 16 : states + 24, 0:bc_cols]
    bc_acc_ref = carry_ref.at[states + 24 : states + 32, 0:bc_cols]
    head_ref = carry_ref.at[states + 32 : states + 32 + 2 * HEAD_ROWS, 0:CHUNK]

    @pl.when(step_id == 0)
    def _():
        carry_ref[...] = carry_in_ref[...]
        da_rows[...] = jnp.zeros_like(da_rows)

    after_u[CHUNK:, :] = kept_u[...]
    after_bc[CHUNK:, :] = kept_bc[...]
    is_start = jnp.logical_and(is_start_part, step_id == pl.num_programs(0) - 1)
    ext_u[0:8, :] = jnp.where(is_start, 0.0, u_before_ref[...])
    ext_bc[0:8, :] = jnp.where(is_start, 0.0, bc_before_ref[...])
    ext_u[8 : 8 + CHUNK, :] = u_ref[...]
    ext_bc[8 : 8 + CHUNK, :] = bc_ref[...]
    v_x = convolved(ext_u, cx_ref)
    sig_x = sigmoid(v_x)
    x = v_x * sig_x
    v_bc = convolved(ext_bc, cbc_ref)
    sig_bc = sigmoid(v_bc)
    sc = (v_bc * sig_bc).astype(bf16)
    b_low, c_low = sc[:, :states], sc[:, states:]
    raw = dr_ref[...]
    step = softplus(raw + hp_ref[0:1, :])
    decay = -step * jnp.exp(hp_ref[1:2, :])
    rows, columns = at_or_after()
    causal = rows >= columns
    cum = mm_exact(causal.astype(f32), decay)
    cum_t = cum.T
    inner_t = mm(b_low, c_low, NT)
    held_low = h_ref[...]
    carried = mm(c_low, held_low)
    next_grad = state[...]
    next_low = next_grad.astype(bf16)
    from_next = mm(b_low, next_low)
    z = z_ref[...]
    sig_z = sigmoid(z)
    gate = z * sig_z
    dg = dg_ref[...].astype(f32)
    dproj_ref[:, 0:inner_cols] = (
        dg * y_ref[...].astype(f32) * (sig_z * (1.0 + z * (1.0 - sig_z)))
    ).astype(bf16)
    dy = dg * gate
    later = rows <= columns
    reaches = causal.astype(bf16)
    inner_grad = jnp.zeros((CHUNK, CHUNK), f32)
    carry_terms, tail_terms, step_terms, dye_parts, xw_parts, held_terms = [], [], [], [], [], []
    for pair in range(pairs):
        at = slice(pair * LANES, (pair + 1) * LANES)
        x_pair = x[:, at]
        dy_pair = dy[:, at]
        cum_pair = pair_columns(cum, pair)
        last = cum_pair[CHUNK - 1 : CHUNK, :]
        step_pair = pair_columns(step, pair)
        x_step = x_pair * step_pair
        dy_low = dy_pair.astype(bf16)
        both = mm(split_heads(x_step.astype(bf16)), dy_low, NT)
        mixing, products = [], []
        for part, head in enumerate((2 * pair, 2 * pair + 1)):
            spread = cum_t[head : head + 1, :] - cum[:, head : head + 1]
            decayed = jnp.exp(jnp.where(later, spread, masked_score))
            grad_part = decayed * both[part * CHUNK : (part + 1) * CHUNK, :]
            inner_grad = inner_grad + grad_part
            products.append((grad_part * inner_t).astype(bf16))
            mixing.append((decayed * inner_t).astype(bf16))
        reach = mm(jnp.concatenate(products, axis=0), reaches)
        for part, head in enumerate((2 * pair, 2 * pair + 1)):
            block = reach[part * CHUNK : (part + 1) * CHUNK, :]
            da_rows[head : head + 1, :] = jnp.sum(
                jnp.where(rows < columns, block, 0.0), axis=0, keepdims=True
            )
        x_grad = mm(jnp.concatenate(mixing, axis=1), split_heads(dy_low))
        grown = jnp.exp(cum_pair)
        dye = dy_pair * grown
        dye_low = dye.astype(bf16)
        dye_parts.append(dye_low)
        carry_terms.append((dye * carried[:, at]).astype(bf16))
        tail = jnp.exp(last - cum_pair)
        x_tail = tail * from_next[:, at]
        tail_terms.append((x_step * x_tail).astype(bf16))
        xw_parts.append((x_step * tail).astype(bf16))
        x_grad = x_grad + x_tail
        step_terms.append((x_pair * x_grad).astype(bf16))
        skip_gain = pair_columns(hp_ref[2:3, :], pair)
        uc_grad = step_pair * x_grad + skip_gain * dy_pair
        v_pair, s_pair = v_x[:, at], sig_x[:, at]
        after_u[0:CHUNK, at] = uc_grad * (s_pair * (1.0 + v_pair * (1.0 - s_pair)))
        wide_ref[taps + 1 : taps + 2, at] += jnp.sum(dy_pair * x_pair, axis=0, keepdims=True)
        held_scale = jnp.exp(last)
        kept = next_grad[:, at] * held_scale
        held_terms.append(jnp.sum(kept * held_low[:, at].astype(f32), axis=0, keepdims=True))
        state[:, at] = kept
    dye_all = jnp.concatenate(dye_parts, axis=1)
    xw_all = jnp.concatenate(xw_parts, axis=1)
    state[...] += mm(c_low, dye_all, TN)
    inner_grad_low = inner_grad.astype(bf16)
    b_grad = mm(inner_grad_low, c_low) + mm(xw_all, next_low, NT)
    c_grad = mm(inner_grad_low, b_low, TN) + mm(dye_all, held_low, NT)
    sc_grad = jnp.concatenate([b_grad, c_grad], axis=1)
    after_bc[0:CHUNK, :] = sc_grad * (sig_bc * (1.0 + v_bc * (1.0 - sig_bc)))

    head_ids = lax.broadcasted_iota(jnp.int32, (HEAD_ROWS, inner_cols), 0)
    channels = lax.broadcasted_iota(jnp.int32, (HEAD_ROWS, inner_cols), 1)
    members = (lax.div(channels, P_SIZE) == head_ids).astype(bf16)
    carry_row = mm(members, jnp.concatenate(carry_terms, axis=1), NT)
    tail_row = mm(members, jnp.concatenate(tail_terms, axis=1), NT)
    step_row = mm(members, jnp.concatenate(step_terms, axis=1), NT)
    held_row = jnp.concatenate(held_terms, axis=1)
    held_col = jnp.sum(
        jnp.where(lax.div(channels, P_SIZE) == head_ids, held_row, 0.0), axis=1, keepdims=True
    )
    decay_grad = (
        da_rows[...]
        + mm_exact(carry_row, causal.astype(f32))
        + mm_exact(tail_row, (rows < columns).astype(f32))
        + held_col
    )
    raw_t = raw.T[:HEAD_ROWS, :] + hpt_ref[:, 0:1]
    step_t = softplus(raw_t)
    rate = -jnp.exp(hpt_ref[:, 1:2])
    step_grad = step_row + decay_grad * rate
    real = lax.broadcasted_iota(jnp.int32, (HEAD_ROWS, CHUNK), 0) < 2 * pairs
    raw_grad = jnp.where(real, step_grad * sigmoid(raw_t), 0.0)
    head_ref[0:HEAD_ROWS, :] += raw_grad
    head_ref[HEAD_ROWS:, :] += jnp.where(real, decay_grad * rate * step_t, 0.0)
    raw_grad_cols = jnp.concatenate(
        [raw_grad, jnp.zeros((LANES - HEAD_ROWS, CHUNK), f32)], axis=0
    ).T

    base = 2 * inner_cols
    for ext_ref, after_ref, taps_ref, acc_ref, start in (
        (ext_u, after_u, cx_ref, wide_ref, inner_cols),
        (ext_bc, after_bc, cbc_ref, bc_acc_ref, base),
    ):
        width = after_ref.shape[1]
        conv_grad = after_ref[0:CHUNK, :]
        value_grad = after_ref[taps - 1 : taps - 1 + CHUNK, :] * taps_ref[0:1, :]
        for k in range(1, taps):
            shift = taps - 1 - k
            value_grad = value_grad + after_ref[shift : shift + CHUNK, :] * taps_ref[k : k + 1, :]
        dproj_ref[:, start : start + width] = value_grad.astype(bf16)
        for k in range(taps):
            acc_ref[k : k + 1, :] += jnp.sum(
                conv_grad * ext_ref[5 + k : 5 + k + CHUNK, :], axis=0, keepdims=True
            )
        acc_ref[taps : taps + 1, :] += jnp.sum(conv_grad, axis=0, keepdims=True)
    dproj_ref[:, base + bc_cols :] = raw_grad_cols.astype(bf16)
    kept_u[...] = after_u[0:8, :]
    kept_bc[...] = after_bc[0:8, :]


def swap_halves(values):
    half = P_SIZE // 2
    lane = lax.broadcasted_iota(jnp.int32, values.shape, 1)
    first = lax.rem(lane, P_SIZE) < half
    return jnp.where(
        first, pltpu.roll(values, LANES - half, axis=1), pltpu.roll(values, half, axis=1)
    )


def rotated(values, cosine, sine):
    return values * cosine + swap_halves(values) * sine


def rotated_back(values, cosine, sine):
    return values * cosine - swap_halves(values) * sine


def keys_and_values(qkv_ref, cos_ref, sin_ref):
    kv = qkv_ref[:, qkv_ref.shape[1] - LANES :]
    low = low_lanes(kv.shape)
    turned = rotated(kv, cos_ref[...], sin_ref[...])
    keys = jnp.where(low, turned, pltpu.roll(turned, P_SIZE, axis=1)).astype(bf16)
    values = jnp.where(low, pltpu.roll(kv, P_SIZE, axis=1), kv).astype(bf16)
    return keys, values


def score_weights(queries, keys, start):
    scores = mm(queries, keys, NT)
    rows = lax.broadcasted_iota(jnp.int32, scores.shape, 0) + start
    columns = lax.broadcasted_iota(jnp.int32, scores.shape, 1)
    scores = jnp.where(rows >= columns, scores, masked_score)
    weights = jnp.exp(scores - jnp.max(scores, axis=1, keepdims=True))
    return weights * (1.0 / jnp.sum(weights, axis=1, keepdims=True))


def rotated_queries(qkv_ref, cos_ref, sin_ref, here, at):
    turned = rotated(qkv_ref[here, at], cos_ref[here, :], sin_ref[here, :]).astype(bf16)
    return turned * jnp.asarray(P_SIZE**-0.5, bf16)


def attention_forward_kernel(qkv_ref, cos_ref, sin_ref, o_ref):
    keys, values = keys_and_values(qkv_ref, cos_ref, sin_ref)
    for block in range(LEN // QBLOCK):
        here = slice(block * QBLOCK, (block + 1) * QBLOCK)
        seen = (block + 1) * QBLOCK
        for pair in range(o_ref.shape[1] // LANES):
            at = slice(pair * LANES, (pair + 1) * LANES)
            queries = rotated_queries(qkv_ref, cos_ref, sin_ref, here, at)
            low = low_lanes(queries.shape)
            zero = jnp.zeros_like(queries)
            outs = []
            for chosen in (jnp.where(low, queries, zero), jnp.where(low, zero, queries)):
                weights = score_weights(chosen, keys[:seen], block * QBLOCK)
                outs.append(mm(weights.astype(bf16), values[:seen]))
            o_ref[here, at] = jnp.where(low_lanes(outs[0].shape), outs[0], outs[1]).astype(bf16)


def attention_backward_kernel(
    qkv_ref, cos_ref, sin_ref, *rest, parts
):
    grad_ref, key_grad, value_grad = rest[-3:]
    do_refs = rest[:parts]
    keys, values = keys_and_values(qkv_ref, cos_ref, sin_ref)
    key_grad[...] = jnp.zeros_like(key_grad)
    value_grad[...] = jnp.zeros_like(value_grad)
    q_cols = do_refs[0].shape[1]
    block_rows = do_refs[0].shape[0]
    for block in range(LEN // QBLOCK):
        here = slice(block * QBLOCK, (block + 1) * QBLOCK)
        seen = (block + 1) * QBLOCK
        for pair in range(q_cols // LANES):
            at = slice(pair * LANES, (pair + 1) * LANES)
            queries = rotated_queries(qkv_ref, cos_ref, sin_ref, here, at)
            inside = block * QBLOCK % block_rows
            out_grad = do_refs[block * QBLOCK // block_rows][inside : inside + QBLOCK, at]
            low = low_lanes(queries.shape)
            zero = jnp.zeros_like(queries)
            parts = []
            for is_low in (True, False):
                q_one = jnp.where(low, queries, zero) if is_low else jnp.where(low, zero, queries)
                g_one = jnp.where(low, out_grad, zero) if is_low else jnp.where(low, zero, out_grad)
                weights = score_weights(q_one, keys[:seen], block * QBLOCK)
                weight_grad = mm(g_one, values[:seen], NT)
                inner = jnp.sum(weights * weight_grad, axis=1, keepdims=True)
                score_grad = (weights * (weight_grad - inner)).astype(bf16)
                parts.append(mm(score_grad, keys[:seen]))
                key_grad[:seen, :] += mm(score_grad, q_one, TN)
                value_grad[:seen, :] += mm(weights.astype(bf16), g_one, TN)
            turned = jnp.where(low_lanes(parts[0].shape), parts[0], parts[1]) * P_SIZE**-0.5
            grad_ref[here, at] = rotated_back(turned, cos_ref[here, :], sin_ref[here, :]).astype(
                bf16
            )
    keys_sum = key_grad[...]
    keys_sum = keys_sum + pltpu.roll(keys_sum, P_SIZE, axis=1)
    values_sum = value_grad[...]
    values_sum = values_sum + pltpu.roll(values_sum, P_SIZE, axis=1)
    keys_sum = rotated_back(keys_sum, cos_ref[...], sin_ref[...])
    grad_ref[:, q_cols:] = jnp.where(low_lanes(keys_sum.shape), keys_sum, values_sum).astype(bf16)


def rotary_tables():
    half = P_SIZE // 2
    frequency = jnp.exp(jnp.arange(half, dtype=f32) * (-2.0 * math.log(rope_base) / P_SIZE))
    angles = jnp.arange(LEN, dtype=f32)[:, None] * frequency[None, :]
    cosine, sine = jnp.cos(angles), jnp.sin(angles)
    return (
        jnp.concatenate([cosine, cosine, cosine, cosine], axis=1),
        jnp.concatenate([-sine, sine, -sine, sine], axis=1),
    )


def short_kernel():
    return pl.CostEstimate(flops=1000, bytes_accessed=1000, transcendentals=0)


def any_place():
    return pl.BlockSpec(memory_space=pl.ANY)


def vmem_params(megabytes):
    return pltpu.CompilerParams(
        vmem_limit_bytes=megabytes * 1024 * 1024, dimension_semantics=("arbitrary",)
    )


def mixer_forward(proj, conv_x, conv_bc, heads, inner_cols, bc_cols):
    rows_all = proj.shape[0]
    states = bc_cols // 2
    bc_at = 2 * inner_cols // bc_cols
    dt_at = (2 * inner_cols + bc_cols) // LANES
    steps = rows_all // CHUNK
    return pl.pallas_call(
        mixer_forward_kernel,
        grid=(steps,),
        in_specs=[
            pl.BlockSpec((CHUNK, inner_cols), lambda i: (i, 0)),
            pl.BlockSpec((CHUNK, inner_cols), lambda i: (i, 1)),
            pl.BlockSpec((CHUNK, bc_cols), lambda i: (i, bc_at)),
            pl.BlockSpec((CHUNK, LANES), lambda i: (i, dt_at)),
            pl.BlockSpec(conv_x.shape, lambda i: (0, 0)),
            pl.BlockSpec(conv_bc.shape, lambda i: (0, 0)),
            pl.BlockSpec(heads.shape, lambda i: (0, 0)),
        ],
        out_specs=[
            pl.BlockSpec((CHUNK, inner_cols), lambda i: (i, 0)),
            pl.BlockSpec((CHUNK, inner_cols), lambda i: (i, 0)),
            pl.BlockSpec((states, inner_cols), lambda i: (i, 0)),
        ],
        out_shape=[
            jax.ShapeDtypeStruct((rows_all, inner_cols), bf16),
            jax.ShapeDtypeStruct((rows_all, inner_cols), bf16),
            jax.ShapeDtypeStruct((steps * states, inner_cols), bf16),
        ],
        scratch_shapes=[
            pltpu.VMEM((states, inner_cols), f32),
            pltpu.VMEM((CHUNK + 8, inner_cols), f32),
            pltpu.VMEM((CHUNK + 8, bc_cols), f32),
        ],
        compiler_params=vmem_params(32),
        cost_estimate=short_kernel(),
        name="mixer_forward",
    )(proj, proj, proj, proj, conv_x, conv_bc, heads)


def mixer_backward(proj, y, dg, held, carry, whole, part, params, inner_cols, bc_cols, *deps):
    rows_all = proj.shape[0]
    states = bc_cols // 2
    bc_at = 2 * inner_cols // bc_cols
    dt_at = (2 * inner_cols + bc_cols) // LANES
    steps = dg.shape[0] // CHUNK
    per = CHUNK // 8
    grad_cols = 2 * inner_cols + bc_cols + LANES

    def at(i):
        return part * steps + steps - 1 - i

    def before(i):
        return jnp.maximum(at(i) * per - 1, 0)

    held_out = [] if whole is None else [whole]
    earlier = held_out + list(deps)
    return pl.pallas_call(
        functools.partial(mixer_backward_kernel, is_start_part=part == 0),
        grid=(steps,),
        in_specs=[
            pl.BlockSpec((CHUNK, inner_cols), lambda i: (at(i), 0)),
            pl.BlockSpec((CHUNK, inner_cols), lambda i: (at(i), 1)),
            pl.BlockSpec((CHUNK, bc_cols), lambda i: (at(i), bc_at)),
            pl.BlockSpec((CHUNK, LANES), lambda i: (at(i), dt_at)),
            pl.BlockSpec((8, inner_cols), lambda i: (before(i), 1)),
            pl.BlockSpec((8, bc_cols), lambda i: (before(i), bc_at)),
            pl.BlockSpec((CHUNK, inner_cols), lambda i: (at(i), 0)),
            pl.BlockSpec((CHUNK, inner_cols), lambda i: (steps - 1 - i, 0)),
            pl.BlockSpec((states, inner_cols), lambda i: (at(i), 0)),
        ]
        + [pl.BlockSpec(value.shape, lambda i: (0, 0)) for value in params]
        + [pl.BlockSpec(carry.shape, lambda i: (0, 0))]
        + [pl.BlockSpec(memory_space=pl.ANY) for _ in earlier],
        out_specs=[
            pl.BlockSpec((CHUNK, grad_cols), lambda i: (at(i), 0)),
            pl.BlockSpec(carry.shape, lambda i: (0, 0)),
        ],
        out_shape=[
            jax.ShapeDtypeStruct((rows_all, grad_cols), bf16),
            jax.ShapeDtypeStruct(carry.shape, f32),
        ],
        scratch_shapes=[
            pltpu.VMEM((CHUNK + 8, inner_cols), f32),
            pltpu.VMEM((CHUNK + 8, bc_cols), f32),
            pltpu.VMEM((CHUNK + 8, inner_cols), f32),
            pltpu.VMEM((CHUNK + 8, bc_cols), f32),
            pltpu.VMEM((HEAD_ROWS, CHUNK), f32),
        ],
        input_output_aliases={14: 0} if held_out else {},
        compiler_params=vmem_params(48),
        cost_estimate=short_kernel(),
        name="mixer_backward",
    )(proj, proj, proj, proj, proj, proj, y, dg, held, *params, carry, *earlier)


def attention_forward(proj, tables, q_cols):
    rows_all = proj.shape[0]
    cols = q_cols + LANES
    return pl.pallas_call(
        attention_forward_kernel,
        grid=(rows_all // LEN,),
        in_specs=[
            pl.BlockSpec((LEN, cols), lambda i: (i, proj.shape[1] // cols - 1)),
            pl.BlockSpec((LEN, LANES), lambda i: (0, 0)),
            pl.BlockSpec((LEN, LANES), lambda i: (0, 0)),
        ],
        out_specs=pl.BlockSpec((LEN, q_cols), lambda i: (i, 0)),
        out_shape=jax.ShapeDtypeStruct((rows_all, q_cols), bf16),
        compiler_params=vmem_params(40),
        cost_estimate=short_kernel(),
        name="attention_forward",
    )(proj, *tables)


def attention_backward(proj, tables, out_grads, q_cols, *deps):
    rows_all = proj.shape[0]
    cols = q_cols + LANES
    return pl.pallas_call(
        functools.partial(attention_backward_kernel, parts=len(out_grads)),
        grid=(rows_all // LEN,),
        in_specs=[
            pl.BlockSpec((LEN, cols), lambda i: (i, proj.shape[1] // cols - 1)),
            pl.BlockSpec((LEN, LANES), lambda i: (0, 0)),
            pl.BlockSpec((LEN, LANES), lambda i: (0, 0)),
        ]
        + [
            pl.BlockSpec((grad.shape[0], q_cols), lambda i: (0, grad.shape[1] // q_cols - 1))
            for grad in out_grads
        ]
        + [any_place() for _ in deps],
        out_specs=pl.BlockSpec((LEN, cols), lambda i: (i, 0)),
        out_shape=jax.ShapeDtypeStruct((rows_all, cols), bf16),
        scratch_shapes=[pltpu.VMEM((LEN, LANES), f32), pltpu.VMEM((LEN, LANES), f32)],
        compiler_params=vmem_params(48),
        cost_estimate=short_kernel(),
        name="attention_backward",
    )(proj, *tables, *out_grads, *deps)


def feed_forward_kernel(
    x_ref, low_ref, arrived_ref, gain_ref, cot_ref, gate_w_ref, up_w_ref, down_w_ref, *rest
):
    mid_ref, n2_ref, act_ref, gate_grad_ref, up_grad_ref, grad_ref, normed, total = rest[-8:]
    step_id = pl.program_id(0)

    @pl.when(step_id == 0)
    def _():
        mid = x_ref[...].astype(f32) + (low_ref[...].astype(f32) + arrived_ref[...].astype(f32))
        inverse = lax.rsqrt(jnp.mean(mid * mid, axis=-1, keepdims=True) + epsilon)
        mid_ref[...] = mid
        value = (mid * inverse * gain_ref[...]).astype(bf16)
        normed[...] = value
        n2_ref[...] = value
        total[...] = jnp.zeros_like(total)

    n2 = normed[...]
    gate = mm(n2, gate_w_ref[...])
    up = mm(n2, up_w_ref[...])
    sig = sigmoid(gate)
    silu = gate * sig
    act_ref[...] = (silu * up).astype(bf16)
    grad = mm(cot_ref[...], down_w_ref[...])
    gate_grad = (grad * up * (sig * (1.0 + gate * (1.0 - sig)))).astype(bf16)
    up_grad = (grad * silu).astype(bf16)
    gate_grad_ref[...] = gate_grad
    up_grad_ref[...] = up_grad
    total[...] += mm(gate_grad, gate_w_ref[...], NT) + mm(up_grad, up_w_ref[...], NT)

    @pl.when(step_id == pl.num_programs(0) - 1)
    def _():
        grad_ref[...] = total[...].astype(bf16)


def feed_forward(tokens, low, arrived, gain, cotangent, w_out, buffers, part, *deps):
    rows, width = low.shape
    hidden = w_out.shape[1] // 3
    blocks = hidden // HIDDEN_BLOCK
    here = pl.BlockSpec((rows, width), lambda h: (part, 0))
    only = pl.BlockSpec((rows, width), lambda h: (0, 0))
    block_out = pl.BlockSpec((rows, HIDDEN_BLOCK), lambda h: (part, h))

    def weight(offset):
        return pl.BlockSpec((width, HIDDEN_BLOCK), lambda h: (0, offset * blocks + h))

    whole = tokens.shape[0]
    return pl.pallas_call(
        feed_forward_kernel,
        grid=(blocks,),
        in_specs=[
            here,
            only,
            only,
            pl.BlockSpec((1, width), lambda h: (0, 0)),
            here,
            weight(0),
            weight(1),
            weight(2),
        ]
        + [any_place() for _ in (*buffers, *deps)],
        out_specs=[here, here, block_out, block_out, block_out, only],
        out_shape=[
            jax.ShapeDtypeStruct((whole, width), f32),
            jax.ShapeDtypeStruct((whole, width), bf16),
            jax.ShapeDtypeStruct((whole, hidden), bf16),
            jax.ShapeDtypeStruct((whole, hidden), bf16),
            jax.ShapeDtypeStruct((whole, hidden), bf16),
            jax.ShapeDtypeStruct((rows, width), bf16),
        ],
        scratch_shapes=[pltpu.VMEM((rows, width), bf16), pltpu.VMEM((rows, width), f32)],
        input_output_aliases={8 + i: i for i in range(len(buffers))},
        compiler_params=vmem_params(40),
        cost_estimate=short_kernel(),
        name="feed_forward",
    )(tokens, low, arrived, gain, cotangent, w_out, w_out, w_out, *buffers, *deps)


def branch_grad_kernel(mid_ref, low_ref, arrived_ref, gain_ref, cot_ref, w_ref, *rest):
    hidden_ref, branch_ref, mix_ref = rest[-3:]
    mid = mid_ref[...]
    inverse = lax.rsqrt(jnp.mean(mid * mid, axis=-1, keepdims=True) + epsilon)
    unit = mid * inverse
    low = low_ref[...].astype(f32)
    scaled = (low + arrived_ref[...].astype(f32)) * gain_ref[...]
    inner = jnp.mean(scaled * unit, axis=-1, keepdims=True)
    grad = cot_ref[...].astype(f32) + (scaled - unit * inner) * inverse
    hidden_ref[...] = grad
    rounded = grad.astype(bf16)
    branch_ref[...] = rounded
    mix_ref[...] = mm(rounded, w_ref[...]).astype(bf16)


def branch_grad(mid, low, arrived, gain, cotangent, w_in, buffers, part, *deps):
    rows, width = low.shape
    whole = cotangent.shape[0]
    mix_cols = width
    here = pl.BlockSpec((rows, width), lambda i: (part, 0))
    only = pl.BlockSpec((rows, width), lambda i: (0, 0))
    row = pl.BlockSpec((1, width), lambda i: (0, 0))
    return pl.pallas_call(
        branch_grad_kernel,
        grid=(1,),
        in_specs=[here, only, only, row, here, pl.BlockSpec(w_in.shape, lambda i: (0, 0))]
        + [any_place() for _ in (*buffers, *deps)],
        out_specs=[here, here, pl.BlockSpec((rows, mix_cols), lambda i: (0, 0))],
        out_shape=[
            jax.ShapeDtypeStruct((whole, width), f32),
            jax.ShapeDtypeStruct((whole, width), bf16),
            jax.ShapeDtypeStruct((rows, mix_cols), bf16),
        ],
        input_output_aliases={6 + i: i for i in range(len(buffers))},
        compiler_params=vmem_params(32),
        cost_estimate=short_kernel(),
        name="branch_grad",
    )(mid, low, arrived, gain, cotangent, w_in, *buffers, *deps)


def weight_grad_kernel(left_ref, right_ref, *rest, has_arrived):
    total = mm(left_ref[...], right_ref[...])
    if has_arrived:
        total = (total + rest[0][...].astype(f32)).astype(bf16)
        rows = total.shape[0] // 2
        rest[-2][...] = total[:rows]
        rest[-1][...] = total[rows:]
    else:
        rest[-1][...] = total.astype(bf16)


def weight_grad(
    left, half, right, right_start, right_cols, buffers, start, columns, arrived, deps
):
    block = 384 if right_cols % 384 == 0 else 256
    offset = right_start // block
    rows, tokens = left.shape
    if half is not None:
        rows //= 2
    first = start // block
    extra = [] if arrived is None else [arrived]
    outs = 1 + len(extra)
    return pl.pallas_call(
        functools.partial(weight_grad_kernel, has_arrived=arrived is not None),
        grid=(right_cols // block,),
        in_specs=[
            pl.BlockSpec((rows, tokens), lambda n: (half or 0, 0)),
            pl.BlockSpec((tokens, block), lambda n: (0, offset + n)),
        ]
        + [pl.BlockSpec((rows, block), lambda n: (0, first + n)) for _ in extra]
        + [any_place() for _ in (*buffers, *deps)],
        out_specs=[pl.BlockSpec((rows // outs, block), lambda n: (0, first + n))] * outs,
        out_shape=[jax.ShapeDtypeStruct((rows // outs, columns), bf16)] * outs,
        input_output_aliases={2 + len(extra) + i: i for i in range(len(buffers))},
        compiler_params=vmem_params(24),
        cost_estimate=short_kernel(),
        name="weight_grad",
    )(left, right, *extra, *buffers, *deps)


def whole(left, right):
    return left, right, 0, right.shape[1]


def weight_grads(pieces, half, arrived=None, deps=(), late=()):
    columns = sum(piece[3] for piece in pieces)
    buffers, start = (), 0
    for left, right, right_start, right_cols in pieces:
        buffers = weight_grad(
            left, half, right, right_start, right_cols, buffers, start, columns, arrived, deps
        )
        deps, late = late, ()
        start += right_cols
    return buffers[0] if arrived is None else buffers


def product_kernel(*refs, count):
    total = mm(refs[0][...], refs[count][...], NT)
    for i in range(1, count):
        total = total + mm(refs[i][...], refs[count + i][...], NT)
    refs[-1][...] = total.astype(bf16)


def product(pairs, *deps):
    rows, out_cols = pairs[0][0].shape[0], pairs[0][1].shape[0]
    block = 256
    return pl.pallas_call(
        functools.partial(product_kernel, count=len(pairs)),
        grid=(out_cols // block,),
        in_specs=[pl.BlockSpec(left.shape, lambda i: (0, 0)) for left, _, _ in pairs]
        + [
            pl.BlockSpec((block, left.shape[1]), lambda i, at=at: (i, at))
            for left, _, at in pairs
        ]
        + [any_place() for _ in deps],
        out_specs=pl.BlockSpec((rows, block), lambda i: (0, i)),
        out_shape=jax.ShapeDtypeStruct((rows, out_cols), bf16),
        compiler_params=vmem_params(32),
        cost_estimate=short_kernel(),
        name="product",
    )(*[left for left, _, _ in pairs], *[right for _, right, _ in pairs], *deps)


def halves_kernel(side_ref, *refs, count):
    total = mm(refs[0][...], refs[count][...], NT)
    for i in range(1, count):
        total = total + mm(refs[i][...], refs[count + i][...], NT)
    there_ref, own_ref, held = refs[-3:]
    held[...] = total.astype(bf16)
    rows = there_ref.shape[0]
    other = pl.multiple_of((1 - side_ref[0]) * rows, rows)
    there_ref[...] = held[pl.ds(other, rows), :]
    own_ref[...] = held[pl.ds(pl.multiple_of(side_ref[0] * rows, rows), rows), :]


def product_halves(side, pairs, *deps):
    rows, out_cols = pairs[0][0].shape[0], pairs[0][1].shape[0]
    block = 256
    return pl.pallas_call(
        functools.partial(halves_kernel, count=len(pairs)),
        grid=(out_cols // block,),
        in_specs=[pl.BlockSpec(memory_space=pltpu.SMEM)]
        + [pl.BlockSpec(left.shape, lambda i: (0, 0)) for left, _, _ in pairs]
        + [
            pl.BlockSpec((block, left.shape[1]), lambda i, at=at: (i, at))
            for left, _, at in pairs
        ]
        + [any_place() for _ in deps],
        out_specs=[pl.BlockSpec((rows // 2, block), lambda i: (0, i))] * 2,
        out_shape=[jax.ShapeDtypeStruct((rows // 2, out_cols), bf16)] * 2,
        scratch_shapes=[pltpu.VMEM((rows, block), bf16)],
        compiler_params=vmem_params(32),
        cost_estimate=short_kernel(),
        name="product_halves",
    )(side, *[left for left, _, _ in pairs], *[right for _, right, _ in pairs], *deps)


def layer_out_kernel(side_ref, mid_ref, own_ref, there_ref, *rest):
    total = own_ref[...].astype(f32) + there_ref[...].astype(f32)
    rest[-1][...] = (mid_ref[...] + total).astype(bf16)


def input_grad_kernel(side_ref, grad_ref, own_ref, there_ref, x_ref, gain_ref, *rest):
    x = x_ref[...].astype(f32)
    inverse = lax.rsqrt(jnp.mean(x * x, axis=-1, keepdims=True) + epsilon)
    unit = x * inverse
    scaled = (own_ref[...].astype(f32) + there_ref[...].astype(f32)) * gain_ref[...]
    inner = jnp.mean(scaled * unit, axis=-1, keepdims=True)
    rest[-1][...] = (grad_ref[...] + (scaled - unit * inner) * inverse).astype(bf16)


def own_rows(kernel, side, whole_parts, parts, row, deps):
    rows, columns = parts[0].shape
    block = 128
    steps = rows // block
    here = pl.BlockSpec((block, columns), lambda i, side: (i, 0))
    mine = pl.BlockSpec((block, columns), lambda i, side: (side[0] * steps + i, 0))
    return pl.pallas_call(
        kernel,
        grid_spec=pltpu.PrefetchScalarGridSpec(
            num_scalar_prefetch=1,
            grid=(steps,),
            in_specs=[mine for _ in whole_parts]
            + [here for _ in parts]
            + [pl.BlockSpec(value.shape, lambda i, side: (0, 0)) for value in row]
            + [any_place() for _ in deps],
            out_specs=here,
        ),
        out_shape=jax.ShapeDtypeStruct((rows, columns), bf16),
        compiler_params=vmem_params(24),
        cost_estimate=short_kernel(),
        name="own_rows",
    )(side, *whole_parts, *parts, *row, *deps)


def inverse_rms(values):
    return lax.rsqrt(jnp.mean(values * values, axis=-1, keepdims=True) + epsilon)


def swap_tensor(values):
    return lax.ppermute(values, "tensor", [(0, 1), (1, 0)])


def swap_dp(values, bit):
    return lax.ppermute(values, "dp", [(i, i ^ bit) for i in range(lax.axis_size("dp"))])


def both_halves(mine):
    other = swap_tensor(mine)
    return jnp.where(
        lax.axis_index("tensor") == 0,
        jnp.concatenate([mine, other], axis=0),
        jnp.concatenate([other, mine], axis=0),
    )


def half_rows(values, index):
    rows = values.shape[0] // 2
    return lax.dynamic_slice_in_dim(values, index * rows, rows, 0)


def after(values, *earlier):
    return pl.pallas_call(
        lambda *refs: None,
        in_specs=[any_place()] * (1 + len(earlier)),
        out_specs=any_place(),
        out_shape=jax.ShapeDtypeStruct(values.shape, values.dtype),
        input_output_aliases={0: 0},
        cost_estimate=short_kernel(),
        name="after",
    )(values, *earlier)


def swap_tensor(values):
    return lax.ppermute(values, "tensor", [(0, 1), (1, 0)])


def swap_dp(values, bit):
    return lax.ppermute(values, "dp", [(i, i ^ bit) for i in range(lax.axis_size("dp"))])


def both_halves(mine):
    other = swap_tensor(mine)
    return jnp.where(
        lax.axis_index("tensor") == 0,
        jnp.concatenate([mine, other], axis=0),
        jnp.concatenate([other, mine], axis=0),
    )


def half_rows(values, index):
    rows = values.shape[0] // 2
    return lax.dynamic_slice_in_dim(values, index * rows, rows, 0)


def chosen_half(parts, index):
    middle = len(parts) // 2
    return jnp.where(
        index == 0,
        jnp.concatenate(parts[:middle], axis=0),
        jnp.concatenate(parts[middle:], axis=0),
    )


def after(values, *earlier):
    return pl.pallas_call(
        lambda *refs: None,
        in_specs=[any_place()] * (1 + len(earlier)),
        out_specs=any_place(),
        out_shape=jax.ShapeDtypeStruct(values.shape, values.dtype),
        input_output_aliases={0: 0},
        cost_estimate=short_kernel(),
        name="after",
    )(values, *earlier)


def sum_far_kernel(own_ref, arrived_ref, *rest):
    rest[-1][...] = (own_ref[...].astype(f32) + arrived_ref[...].astype(f32)).astype(bf16)


def reordering(width):
    dp_count = lax.axis_size("dp")
    here = width // dp_count
    me = lax.axis_index("dp")
    core, near = lax.rem(me, 2), lax.rem(lax.div(me, 2), 2)
    place = jnp.arange(width, dtype=jnp.int32)
    block, inside = place // here, place % here
    quarter, far = block // (dp_count // 4), block % (dp_count // 4)
    block_core = jnp.where(quarter // 2 == 0, 1 - core, core)
    block_near = jnp.where(quarter % 2 == 0, 1 - near, near)
    source = (far * 4 + block_near * 2 + block_core) * here + inside
    return (source[:, None] == jnp.arange(width, dtype=jnp.int32)[None, :]).astype(bf16)


def sum_near(halves):
    there, own = halves
    return own, swap_dp(there, 2)


def sum_far_kernel(me_ref, own_ref, arrived_ref, *rest, far):
    total = (own_ref[...].astype(f32) + arrived_ref[...].astype(f32)).astype(bf16)
    rows = total.shape[0] // far
    scratch = rest[-1]
    scratch[...] = total
    for offset, out_ref in enumerate(rest[-1 - far : -1]):
        place = lax.rem(me_ref[0] + offset, far)
        out_ref[...] = scratch[pl.ds(pl.multiple_of(place * rows, rows), rows), :]


def sum_far(own, arrived, *deps):
    far = lax.axis_size("dp") // 4
    if far > 4:
        return (after((own.astype(f32) + arrived.astype(f32)).astype(bf16), *deps),)
    rows, columns = own.shape
    me = lax.div(lax.axis_index("dp"), 4).reshape(1)
    only = pl.BlockSpec((rows, columns), lambda i: (0, 0))
    return pl.pallas_call(
        functools.partial(sum_far_kernel, far=far),
        grid=(1,),
        in_specs=[pl.BlockSpec(memory_space=pltpu.SMEM), only, only]
        + [any_place() for _ in deps],
        out_specs=[pl.BlockSpec((rows // far, columns), lambda i: (0, 0))] * far,
        out_shape=[jax.ShapeDtypeStruct((rows // far, columns), bf16)] * far,
        scratch_shapes=[pltpu.VMEM((rows, columns), bf16)],
        compiler_params=vmem_params(24),
        cost_estimate=short_kernel(),
        name="sum_far",
    )(me, own, arrived, *deps)


def send_far(blocks):
    far = lax.axis_size("dp") // 4
    if far > 4:
        groups = [[low + 4 * i for i in range(far)] for low in range(4)]
        summed = blocks[0].reshape(far, blocks[0].shape[0] // far, blocks[0].shape[1])
        return [lax.all_to_all(summed, "dp", 0, 0, tiled=True, axis_index_groups=groups)]
    arrived = []
    for offset in range(1, far):
        moves = [(i, (i + 4 * offset) % (4 * far)) for i in range(4 * far)]
        arrived.append(lax.ppermute(blocks[offset], "dp", moves))
    return arrived


def sum_last(blocks, arrived, *deps):
    if arrived[0].ndim == 3:
        return jnp.sum(after(arrived[0], *deps).astype(f32), axis=0)
    total = after(blocks[0], *deps, *arrived).astype(f32)
    for values in arrived:
        total = total + values.astype(f32)
    return total


def add_kernel(left_ref, right_ref, *rest):
    rest[-1][...] = left_ref[...] + right_ref[...]


def added(left, right, *deps):
    only = pl.BlockSpec(left.shape, lambda i: (0, 0))
    return pl.pallas_call(
        add_kernel,
        grid=(1,),
        in_specs=[only, only] + [any_place() for _ in deps],
        out_specs=only,
        out_shape=jax.ShapeDtypeStruct(left.shape, left.dtype),
        compiler_params=vmem_params(16),
        cost_estimate=short_kernel(),
        name="added",
    )(left, right, *deps)


def local(
    tokens,
    gains,
    w_zx,
    w_bc,
    w_dt,
    conv_x,
    conv_bc,
    head_params,
    w_mo,
    w_q,
    w_kv,
    w_ao,
    w_gu,
    w_down,
    cotangent,
):
    dp_count = lax.axis_size("dp")
    side = lax.axis_index("tensor")
    width = tokens.shape[1]
    here = width // dp_count
    inner_cols, bc_cols, head_cols = w_zx.shape[2], w_bc.shape[1], w_dt.shape[1]
    q_cols, kv_cols = w_q.shape[1], 2 * w_kv.shape[2]
    hidden, mo_cols, ao_cols = w_gu.shape[2], w_mo.shape[0], w_ao.shape[0]
    bc_start = 2 * inner_cols
    dt_start = bc_start + bc_cols
    q_start = dt_start + LANES
    kv_start = q_start + q_cols
    in_cols = kv_start + kv_cols

    shared = both_halves(jnp.concatenate([w_bc, gains.T], axis=1))
    in_pack = jnp.concatenate(
        [
            w_zx[:, 0],
            w_zx[:, 1],
            shared[:, :bc_cols],
            w_dt,
            shared[:, bc_cols:],
            jnp.zeros((here, LANES - head_cols - 2), bf16),
            w_q,
            w_kv.reshape(here, kv_cols),
            w_mo.T,
            w_ao.T,
        ],
        axis=1,
    )
    w_in = lax.all_gather(in_pack, "dp", axis=0, tiled=True)
    out_pack = jnp.concatenate([w_gu.reshape(here, 2 * hidden), w_down.T], axis=1)
    tokens_all = both_halves(tokens)
    cotangent_all = both_halves(cotangent)
    out_pack = after(out_pack, w_in, tokens_all, cotangent_all)
    w_out = lax.all_gather(out_pack, "dp", axis=0, tiled=True)
    tables = rotary_tables()
    order = reordering(width)
    unchanged = jnp.eye(width, dtype=bf16)
    kept_rows = width // 2

    mix_full = w_in[:, in_cols:]
    gain_full = w_in[:, dt_start + head_cols : dt_start + head_cols + 2].T.astype(f32)
    gain_one, gain_two = gain_full[0:1], gain_full[1:2]
    heads = jnp.pad(head_params, ((0, 5), (0, LANES - head_cols)))
    mixer_params = (conv_x, conv_bc, heads, heads[:, :HEAD_ROWS].T)

    seq_in = tokens_all.astype(f32)
    inverse_one = inverse_rms(seq_in)
    n1 = (seq_in * inverse_one * gain_one).astype(bf16)
    proj = mm(n1, w_in[:, :in_cols])
    gated, y, held = mixer_forward(proj, conv_x, conv_bc, heads, inner_cols, bc_cols)
    attended = attention_forward(proj, tables, q_cols)

    rows = tokens_all.shape[0] // ROW_PARTS
    backward_parts = list(range(ROW_PARTS))[::-1]
    branch_low, branch_arrived = {}, {}
    for part in backward_parts:
        at = slice(part * rows, (part + 1) * rows)
        branch_low[part] = (
            mm(gated[at], mix_full[:, :mo_cols], NT) + mm(attended[at], mix_full[:, mo_cols:], NT)
        ).astype(bf16)
        branch_arrived[part] = swap_tensor(branch_low[part])
    n1_ordered = product([(order, n1, 0)])
    cotangent_turned = product([(unchanged, cotangent_all, 0)])
    start = backward_parts[0]
    ready = (n1_ordered, cotangent_turned, mix_full)

    n2_grad_low, n2_grad_arrived = {}, {}
    buffers = ()
    for part in backward_parts:
        *buffers, grad_low = feed_forward(
            tokens_all,
            branch_low[part],
            branch_arrived[part],
            gain_two,
            cotangent_all,
            w_out,
            buffers,
            part,
            *ready,
        )
        ready = ()
        n2_grad_low[part] = grad_low
        n2_grad_arrived[part] = swap_tensor(grad_low)
    hidden_one, n2, activated, gate_grad, up_grad = buffers
    n2_turned = product([(unchanged, n2, 0)])
    ffn_pieces = [
        whole(n2_turned, gate_grad),
        whole(n2_turned, up_grad),
        whole(cotangent_turned, activated),
    ]
    ffn_all = weight_grads(ffn_pieces, None, late=(n2_grad_arrived[start],))
    ffn_sum = lax.psum_scatter(ffn_all, "dp", scatter_dimension=0, tiled=True)

    mix_grad = {}
    buffers, proj_grad = (), None
    carry = jnp.zeros((bc_cols // 2 + 32 + 2 * HEAD_ROWS, inner_cols), f32)
    step = ffn_all
    last = backward_parts[-1]
    for part in backward_parts:
        *buffers, mix_grad[part] = branch_grad(
            hidden_one,
            n2_grad_low[part],
            n2_grad_arrived[part],
            gain_two,
            cotangent_all,
            mix_full,
            buffers,
            part,
            step,
        )
        deps = ()
        if part == last:
            ffn_low = product([(activated, w_out, 2)], buffers[1])
            ffn_there = swap_tensor(half_rows(ffn_low, 1 - side))
            branch_ordered = product([(order, buffers[1], 0)], ffn_low)
            mix_pieces = [whole(branch_ordered, gated), whole(branch_ordered, attended)]
            mix_sent = weight_grads(mix_pieces, 0)
            mix_arrived = swap_dp(mix_sent, 1)
            out_grads = [mix_grad[each] for each in range(ROW_PARTS)]
            att_grad = attention_backward(proj, tables, out_grads, q_cols, mix_sent)
            att_pieces = [whole(n1_ordered, att_grad)]
            att_sent = weight_grads(att_pieces, 0)
            att_arrived = swap_dp(att_sent, 1)
            mix_near = sum_near(weight_grads(mix_pieces, 1, mix_arrived, (att_sent,)))
            att_near = sum_near(weight_grads(att_pieces, 1, att_arrived, (mix_near[0],)))
            deps = (att_near[0], ffn_there)
        proj_grad, carry = mixer_backward(
            proj,
            y,
            mix_grad[part],
            held,
            carry,
            proj_grad,
            part,
            mixer_params,
            inner_cols,
            bc_cols,
            *deps,
        )
        step = carry

    sums = carry[bc_cols // 2 + 8 :]
    sums_arrived = swap_dp(sums, 1)
    mix_step = sum_far(*mix_near, carry)
    mix_far = send_far(mix_step)
    att_step = sum_far(*att_near, mix_step[0])
    att_far = send_far(att_step)
    wide_cols = inner_cols + inner_cols // 2
    second_cols = q_start - wide_cols
    first_pieces = [(n1_ordered, proj_grad, 0, wide_cols)]
    second_pieces = [(n1_ordered, proj_grad, wide_cols, second_cols)]
    first_sent = weight_grads(first_pieces, 0, deps=(att_step[0],))
    first_arrived = swap_dp(first_sent, 1)
    second_sent = weight_grads(second_pieces, 0, deps=(first_sent,))
    second_arrived = swap_dp(second_sent, 1)
    sums = added(sums, sums_arrived, second_sent)
    sums_arrived = swap_dp(sums, 2)
    first_near = sum_near(weight_grads(first_pieces, 1, first_arrived, (sums,)))
    second_near = sum_near(weight_grads(second_pieces, 1, second_arrived, (first_near[0],)))
    sums = added(sums, sums_arrived, second_near[0])
    sums_arrived = swap_dp(sums, 4)
    n1_there, n1_own = product_halves(
        side.reshape(1),
        [(proj_grad, w_in, 0), (att_grad, w_in, q_start // (in_cols - q_start))],
        sums,
        *mix_far,
        *att_far,
    )
    n1_arrived = swap_tensor(n1_there)
    sums = added(sums, sums_arrived, n1_own)
    bit = 8
    while bit < dp_count // 2:
        sums = added(sums, swap_dp(sums, bit))
        bit *= 2
    sums_arrived = swap_dp(sums, bit)
    first_step = sum_far(*first_near, sums)
    first_far = send_far(first_step)
    layer_out = own_rows(
        layer_out_kernel, side.reshape(1), [hidden_one, ffn_low], [ffn_there], [], [first_step[0]]
    )
    sums = added(sums, sums_arrived, layer_out)
    second_step = sum_far(*second_near, sums, *first_far)
    second_far = send_far(second_step)
    input_grad = own_rows(
        input_grad_kernel,
        side.reshape(1),
        [buffers[0]],
        [n1_own, n1_arrived, tokens],
        [gain_one],
        [second_step[0]],
    )
    ffn_sum = after(ffn_sum, input_grad, *second_far).astype(f32)
    mix_sum = sum_last(mix_step, mix_far, input_grad, *second_far)
    att_sum = sum_last(att_step, att_far, input_grad, *second_far)
    first_sum = sum_last(first_step, first_far, input_grad, *second_far)
    second_sum = sum_last(second_step, second_far, input_grad)

    taps = conv_x.shape[0]
    grad_conv_x = sums[:taps]
    conv_bc_half = sums[16 : 16 + taps, :bc_cols]
    head_sums = jnp.sum(sums[24:, :CHUNK], axis=1)
    grad_head = jnp.stack(
        [
            head_sums[:head_cols],
            head_sums[HEAD_ROWS : HEAD_ROWS + head_cols],
            jnp.sum(sums[taps].reshape(head_cols, P_SIZE), axis=1),
        ]
    )

    in_low = in_pack.astype(f32)
    gain_one_grad = (
        jnp.sum(in_low[:, :wide_cols] * first_sum, axis=1)
        + jnp.sum(in_low[:, wide_cols:q_start] * second_sum[:, :second_cols], axis=1)
        + jnp.sum(in_low[:, q_start:in_cols] * att_sum, axis=1)
    ) / shared[:, bc_cols].astype(f32)
    gain_two_grad = jnp.sum(
        out_pack[:, : 2 * hidden].astype(f32) * ffn_sum[:, : 2 * hidden], axis=1
    ) / shared[:, bc_cols + 1].astype(f32)
    shared_half = jnp.concatenate(
        [
            second_sum[:, bc_start - wide_cols : dt_start - wide_cols],
            jnp.stack([gain_one_grad, gain_two_grad], axis=1),
        ],
        axis=1,
    )
    to_send = jnp.concatenate(
        [half_rows(shared_half, 1 - side).reshape(-1), conv_bc_half.reshape(-1)]
    )
    arrived = swap_tensor(to_send)
    shared_sum = half_rows(shared_half, side) + arrived[: shared_half.size // 2].reshape(
        here // 2, bc_cols + 2
    )
    grad_conv_bc = conv_bc_half + arrived[shared_half.size // 2 :].reshape(taps, bc_cols)
    return (
        layer_out,
        input_grad,
        shared_sum[:, bc_cols:].T,
        jnp.concatenate([first_sum, second_sum[:, : bc_start - wide_cols]], axis=1).reshape(
            here, 2, inner_cols
        ),
        shared_sum[:, :bc_cols],
        second_sum[:, dt_start - wide_cols : dt_start - wide_cols + head_cols],
        grad_conv_x,
        grad_conv_bc,
        grad_head,
        mix_sum[:, :mo_cols].T,
        att_sum[:, :q_cols],
        att_sum[:, q_cols:].reshape(here, 2, kv_cols // 2),
        mix_sum[:, mo_cols:].T,
        ffn_sum[:, : 2 * hidden].reshape(here, 2, hidden),
        ffn_sum[:, 2 * hidden :].T,
    )


def solution(mesh):
    placed = (
        P(("dp", "tensor"), None),
        P(None, ("dp", "tensor")),
        P("dp", None, "tensor"),
        P(("dp", "tensor"), None),
        P("dp", "tensor"),
        P(None, "tensor"),
        P(),
        P(None, "tensor"),
        P("tensor", "dp"),
        P("dp", "tensor"),
        P("dp", None, "tensor"),
        P("tensor", "dp"),
        P("dp", None, "tensor"),
        P("tensor", "dp"),
        P(("dp", "tensor"), None),
    )
    return jax.shard_map(
        local,
        mesh=mesh,
        in_specs=placed,
        out_specs=(
            P(("dp", "tensor"), None),
            P(("dp", "tensor"), None),
            P(None, ("dp", "tensor")),
            P("dp", None, "tensor"),
            P(("dp", "tensor"), None),
            P("dp", "tensor"),
            P(None, "tensor"),
            P(),
            P(None, "tensor"),
            P("tensor", "dp"),
            P("dp", "tensor"),
            P("dp", None, "tensor"),
            P("tensor", "dp"),
            P("dp", None, "tensor"),
            P("tensor", "dp"),
        ),
        check_vma=False,
    )
```

```python
import functools
import math

import jax
import jax.numpy as jnp
from jax import lax
from jax.experimental import pallas as pl
from jax.experimental.pallas import tpu as pltpu
from jax.sharding import PartitionSpec as P

P_SIZE = 64
LEN = 1024
CHUNK = 128
LANES = 128
QBLOCK = 256
HEAD_ROWS = 16
ROW_PARTS = 2
HIDDEN_BLOCK = 512

highest = lax.Precision.HIGHEST
epsilon = 1e-05
rope_base = 100000000000.0
masked_score = -1e30
f32 = jnp.float32
bf16 = jnp.bfloat16

NN = (((1,), (0,)), ((), ()))
NT = (((1,), (1,)), ((), ()))
TN = (((0,), (0,)), ((), ()))
TT = (((0,), (1,)), ((), ()))


def mm(left, right, dims=NN):
    return lax.dot_general(left, right, dims, preferred_element_type=f32)


def mm_exact(left, right, dims=NN):
    return lax.dot_general(left, right, dims, precision=highest, preferred_element_type=f32)


def low_lanes(shape):
    return lax.broadcasted_iota(jnp.int32, shape, 1) < P_SIZE


def softplus(values):
    return jnp.maximum(values, 0.0) + jnp.log1p(jnp.exp(-jnp.abs(values)))


def sigmoid(values):
    return 1.0 / (1.0 + jnp.exp(-values))


def at_or_after():
    rows = lax.broadcasted_iota(jnp.int32, (CHUNK, CHUNK), 0)
    columns = lax.broadcasted_iota(jnp.int32, (CHUNK, CHUNK), 1)
    return rows, columns


def convolved(ext_ref, taps_ref):
    taps = taps_ref.shape[0] - 1
    total = taps_ref[taps : taps + 1, :] + ext_ref[5 : 5 + CHUNK, :] * taps_ref[0:1, :]
    for k in range(1, taps):
        total = total + ext_ref[5 + k : 5 + k + CHUNK, :] * taps_ref[k : k + 1, :]
    return total


def pair_columns(table, pair):
    low = low_lanes((table.shape[0], LANES))
    return jnp.where(low, table[:, 2 * pair : 2 * pair + 1], table[:, 2 * pair + 1 : 2 * pair + 2])


def split_heads(values):
    low = low_lanes(values.shape)
    zero = jnp.zeros_like(values)
    return jnp.concatenate([jnp.where(low, values, zero), jnp.where(low, zero, values)], axis=0)


def mixer_forward_kernel(
    z_ref, u_ref, bc_ref, dr_ref, cx_ref, cbc_ref, hp_ref, g_ref, y_ref, h_ref, state, ext_u, ext_bc
):
    chunks = LEN // CHUNK
    first = lax.rem(pl.program_id(0), chunks) == 0
    pairs = u_ref.shape[1] // LANES
    states = bc_ref.shape[1] // 2

    @pl.when(first)
    def _():
        state[...] = jnp.zeros_like(state)
        ext_u[0:8, :] = jnp.zeros_like(ext_u[0:8, :])
        ext_bc[0:8, :] = jnp.zeros_like(ext_bc[0:8, :])

    @pl.when(jnp.logical_not(first))
    def _():
        ext_u[0:8, :] = ext_u[CHUNK : CHUNK + 8, :]
        ext_bc[0:8, :] = ext_bc[CHUNK : CHUNK + 8, :]

    ext_u[8 : 8 + CHUNK, :] = u_ref[...]
    ext_bc[8 : 8 + CHUNK, :] = bc_ref[...]
    v_x = convolved(ext_u, cx_ref)
    x = v_x * sigmoid(v_x)
    v_bc = convolved(ext_bc, cbc_ref)
    sc = (v_bc * sigmoid(v_bc)).astype(bf16)
    b_low, c_low = sc[:, :states], sc[:, states:]
    step = softplus(dr_ref[...] + hp_ref[0:1, :])
    decay = -step * jnp.exp(hp_ref[1:2, :])
    rows, columns = at_or_after()
    causal = rows >= columns
    cum = mm_exact(causal.astype(f32), decay)
    cum_t = cum.T
    inner = mm(c_low, b_low, NT)
    held = state[...]
    held_low = held.astype(bf16)
    h_ref[...] = held_low
    carried = mm(c_low, held_low)
    z = z_ref[...]
    gate = z * sigmoid(z)
    fresh = []
    for pair in range(pairs):
        at = slice(pair * LANES, (pair + 1) * LANES)
        x_pair = x[:, at]
        cum_pair = pair_columns(cum, pair)
        last = cum_pair[CHUNK - 1 : CHUNK, :]
        x_step = x_pair * pair_columns(step, pair)
        mixing = []
        for head in (2 * pair, 2 * pair + 1):
            spread = cum[:, head : head + 1] - cum_t[head : head + 1, :]
            mixing.append((jnp.exp(jnp.where(causal, spread, masked_score)) * inner).astype(bf16))
        out = mm(jnp.concatenate(mixing, axis=1), split_heads(x_step.astype(bf16)))
        out = out + carried[:, at] * jnp.exp(cum_pair)
        out = out + pair_columns(hp_ref[2:3, :], pair) * x_pair
        y_ref[:, at] = out.astype(bf16)
        g_ref[:, at] = (out * gate[:, at]).astype(bf16)
        fresh.append((x_step * jnp.exp(last - cum_pair)).astype(bf16))
        held_scale = jnp.exp(last)
        state[:, at] = held[:, at] * held_scale
    state[...] += mm(b_low, jnp.concatenate(fresh, axis=1), TN)


def mixer_backward_kernel(
    z_ref,
    u_ref,
    bc_ref,
    dr_ref,
    u_before_ref,
    bc_before_ref,
    y_ref,
    dg_ref,
    h_ref,
    cx_ref,
    cbc_ref,
    hp_ref,
    hpt_ref,
    carry_in_ref,
    *rest,
    is_start_part,
):
    dproj_ref, carry_ref, ext_u, ext_bc, after_u, after_bc, da_rows = rest[-7:]
    step_id = pl.program_id(0)
    inner_cols = u_ref.shape[1]
    bc_cols = bc_ref.shape[1]
    pairs = inner_cols // LANES
    states = bc_cols // 2
    taps = cx_ref.shape[0] - 1
    state = carry_ref.at[0:states, :]
    kept_u = carry_ref.at[states : states + 8, :]
    wide_ref = carry_ref.at[states + 8 : states + 16, :]
    kept_bc = carry_ref.at[states + 16 : states + 24, 0:bc_cols]
    bc_acc_ref = carry_ref.at[states + 24 : states + 32, 0:bc_cols]
    head_ref = carry_ref.at[states + 32 : states + 32 + 2 * HEAD_ROWS, 0:CHUNK]

    @pl.when(step_id == 0)
    def _():
        carry_ref[...] = carry_in_ref[...]
        da_rows[...] = jnp.zeros_like(da_rows)

    after_u[CHUNK:, :] = kept_u[...]
    after_bc[CHUNK:, :] = kept_bc[...]
    is_start = jnp.logical_and(is_start_part, step_id == pl.num_programs(0) - 1)
    ext_u[0:8, :] = jnp.where(is_start, 0.0, u_before_ref[...])
    ext_bc[0:8, :] = jnp.where(is_start, 0.0, bc_before_ref[...])
    ext_u[8 : 8 + CHUNK, :] = u_ref[...]
    ext_bc[8 : 8 + CHUNK, :] = bc_ref[...]
    v_x = convolved(ext_u, cx_ref)
    sig_x = sigmoid(v_x)
    x = v_x * sig_x
    v_bc = convolved(ext_bc, cbc_ref)
    sig_bc = sigmoid(v_bc)
    sc = (v_bc * sig_bc).astype(bf16)
    b_low, c_low = sc[:, :states], sc[:, states:]
    raw = dr_ref[...]
    step = softplus(raw + hp_ref[0:1, :])
    decay = -step * jnp.exp(hp_ref[1:2, :])
    rows, columns = at_or_after()
    causal = rows >= columns
    cum = mm_exact(causal.astype(f32), decay)
    cum_t = cum.T
    inner_t = mm(b_low, c_low, NT)
    held_low = h_ref[...]
    carried = mm(c_low, held_low)
    next_grad = state[...]
    next_low = next_grad.astype(bf16)
    from_next = mm(b_low, next_low)
    z = z_ref[...]
    sig_z = sigmoid(z)
    gate = z * sig_z
    dg = dg_ref[...].astype(f32)
    dproj_ref[:, 0:inner_cols] = (
        dg * y_ref[...].astype(f32) * (sig_z * (1.0 + z * (1.0 - sig_z)))
    ).astype(bf16)
    dy = dg * gate
    later = rows <= columns
    reaches = causal.astype(bf16)
    inner_grad = jnp.zeros((CHUNK, CHUNK), f32)
    carry_terms, tail_terms, step_terms, dye_parts, xw_parts, held_terms = [], [], [], [], [], []
    for pair in range(pairs):
        at = slice(pair * LANES, (pair + 1) * LANES)
        x_pair = x[:, at]
        dy_pair = dy[:, at]
        cum_pair = pair_columns(cum, pair)
        last = cum_pair[CHUNK - 1 : CHUNK, :]
        step_pair = pair_columns(step, pair)
        x_step = x_pair * step_pair
        dy_low = dy_pair.astype(bf16)
        both = mm(split_heads(x_step.astype(bf16)), dy_low, NT)
        mixing, products = [], []
        for part, head in enumerate((2 * pair, 2 * pair + 1)):
            spread = cum_t[head : head + 1, :] - cum[:, head : head + 1]
            decayed = jnp.exp(jnp.where(later, spread, masked_score))
            grad_part = decayed * both[part * CHUNK : (part + 1) * CHUNK, :]
            inner_grad = inner_grad + grad_part
            products.append((grad_part * inner_t).astype(bf16))
            mixing.append((decayed * inner_t).astype(bf16))
        reach = mm(jnp.concatenate(products, axis=0), reaches)
        for part, head in enumerate((2 * pair, 2 * pair + 1)):
            block = reach[part * CHUNK : (part + 1) * CHUNK, :]
            da_rows[head : head + 1, :] = jnp.sum(
                jnp.where(rows < columns, block, 0.0), axis=0, keepdims=True
            )
        x_grad = mm(jnp.concatenate(mixing, axis=1), split_heads(dy_low))
        grown = jnp.exp(cum_pair)
        dye = dy_pair * grown
        dye_low = dye.astype(bf16)
        dye_parts.append(dye_low)
        carry_terms.append((dye * carried[:, at]).astype(bf16))
        tail = jnp.exp(last - cum_pair)
        x_tail = tail * from_next[:, at]
        tail_terms.append((x_step * x_tail).astype(bf16))
        xw_parts.append((x_step * tail).astype(bf16))
        x_grad = x_grad + x_tail
        step_terms.append((x_pair * x_grad).astype(bf16))
        skip_gain = pair_columns(hp_ref[2:3, :], pair)
        uc_grad = step_pair * x_grad + skip_gain * dy_pair
        v_pair, s_pair = v_x[:, at], sig_x[:, at]
        after_u[0:CHUNK, at] = uc_grad * (s_pair * (1.0 + v_pair * (1.0 - s_pair)))
        wide_ref[taps + 1 : taps + 2, at] += jnp.sum(dy_pair * x_pair, axis=0, keepdims=True)
        held_scale = jnp.exp(last)
        kept = next_grad[:, at] * held_scale
        held_terms.append(jnp.sum(kept * held_low[:, at].astype(f32), axis=0, keepdims=True))
        state[:, at] = kept
    dye_all = jnp.concatenate(dye_parts, axis=1)
    xw_all = jnp.concatenate(xw_parts, axis=1)
    state[...] += mm(c_low, dye_all, TN)
    inner_grad_low = inner_grad.astype(bf16)
    b_grad = mm(inner_grad_low, c_low) + mm(xw_all, next_low, NT)
    c_grad = mm(inner_grad_low, b_low, TN) + mm(dye_all, held_low, NT)
    sc_grad = jnp.concatenate([b_grad, c_grad], axis=1)
    after_bc[0:CHUNK, :] = sc_grad * (sig_bc * (1.0 + v_bc * (1.0 - sig_bc)))

    head_ids = lax.broadcasted_iota(jnp.int32, (HEAD_ROWS, inner_cols), 0)
    channels = lax.broadcasted_iota(jnp.int32, (HEAD_ROWS, inner_cols), 1)
    members = (lax.div(channels, P_SIZE) == head_ids).astype(bf16)
    carry_row = mm(members, jnp.concatenate(carry_terms, axis=1), NT)
    tail_row = mm(members, jnp.concatenate(tail_terms, axis=1), NT)
    step_row = mm(members, jnp.concatenate(step_terms, axis=1), NT)
    held_row = jnp.concatenate(held_terms, axis=1)
    held_col = jnp.sum(
        jnp.where(lax.div(channels, P_SIZE) == head_ids, held_row, 0.0), axis=1, keepdims=True
    )
    decay_grad = (
        da_rows[...]
        + mm_exact(carry_row, causal.astype(f32))
        + mm_exact(tail_row, (rows < columns).astype(f32))
        + held_col
    )
    raw_t = raw.T[:HEAD_ROWS, :] + hpt_ref[:, 0:1]
    step_t = softplus(raw_t)
    rate = -jnp.exp(hpt_ref[:, 1:2])
    step_grad = step_row + decay_grad * rate
    real = lax.broadcasted_iota(jnp.int32, (HEAD_ROWS, CHUNK), 0) < 2 * pairs
    raw_grad = jnp.where(real, step_grad * sigmoid(raw_t), 0.0)
    head_ref[0:HEAD_ROWS, :] += raw_grad
    head_ref[HEAD_ROWS:, :] += jnp.where(real, decay_grad * rate * step_t, 0.0)
    raw_grad_cols = jnp.concatenate(
        [raw_grad, jnp.zeros((LANES - HEAD_ROWS, CHUNK), f32)], axis=0
    ).T

    base = 2 * inner_cols
    for ext_ref, after_ref, taps_ref, acc_ref, start in (
        (ext_u, after_u, cx_ref, wide_ref, inner_cols),
        (ext_bc, after_bc, cbc_ref, bc_acc_ref, base),
    ):
        width = after_ref.shape[1]
        conv_grad = after_ref[0:CHUNK, :]
        value_grad = after_ref[taps - 1 : taps - 1 + CHUNK, :] * taps_ref[0:1, :]
        for k in range(1, taps):
            shift = taps - 1 - k
            value_grad = value_grad + after_ref[shift : shift + CHUNK, :] * taps_ref[k : k + 1, :]
        dproj_ref[:, start : start + width] = value_grad.astype(bf16)
        for k in range(taps):
            acc_ref[k : k + 1, :] += jnp.sum(
                conv_grad * ext_ref[5 + k : 5 + k + CHUNK, :], axis=0, keepdims=True
            )
        acc_ref[taps : taps + 1, :] += jnp.sum(conv_grad, axis=0, keepdims=True)
    dproj_ref[:, base + bc_cols :] = raw_grad_cols.astype(bf16)
    kept_u[...] = after_u[0:8, :]
    kept_bc[...] = after_bc[0:8, :]


def swap_halves(values):
    half = P_SIZE // 2
    lane = lax.broadcasted_iota(jnp.int32, values.shape, 1)
    first = lax.rem(lane, P_SIZE) < half
    return jnp.where(
        first, pltpu.roll(values, LANES - half, axis=1), pltpu.roll(values, half, axis=1)
    )


def rotated(values, cosine, sine):
    return values * cosine + swap_halves(values) * sine


def rotated_back(values, cosine, sine):
    return values * cosine - swap_halves(values) * sine


def keys_and_values(qkv_ref, cos_ref, sin_ref):
    kv = qkv_ref[:, qkv_ref.shape[1] - LANES :]
    low = low_lanes(kv.shape)
    turned = rotated(kv, cos_ref[...], sin_ref[...])
    keys = jnp.where(low, turned, pltpu.roll(turned, P_SIZE, axis=1)).astype(bf16)
    values = jnp.where(low, pltpu.roll(kv, P_SIZE, axis=1), kv).astype(bf16)
    return keys, values


def score_weights(queries, keys, start):
    scores = mm(queries, keys, NT)
    rows = lax.broadcasted_iota(jnp.int32, scores.shape, 0) + start
    columns = lax.broadcasted_iota(jnp.int32, scores.shape, 1)
    scores = jnp.where(rows >= columns, scores, masked_score)
    weights = jnp.exp(scores - jnp.max(scores, axis=1, keepdims=True))
    return weights * (1.0 / jnp.sum(weights, axis=1, keepdims=True))


def rotated_queries(qkv_ref, cos_ref, sin_ref, here, at):
    turned = rotated(qkv_ref[here, at], cos_ref[here, :], sin_ref[here, :]).astype(bf16)
    return turned * jnp.asarray(P_SIZE**-0.5, bf16)


def attention_forward_kernel(qkv_ref, cos_ref, sin_ref, o_ref):
    keys, values = keys_and_values(qkv_ref, cos_ref, sin_ref)
    for block in range(LEN // QBLOCK):
        here = slice(block * QBLOCK, (block + 1) * QBLOCK)
        seen = (block + 1) * QBLOCK
        for pair in range(o_ref.shape[1] // LANES):
            at = slice(pair * LANES, (pair + 1) * LANES)
            queries = rotated_queries(qkv_ref, cos_ref, sin_ref, here, at)
            low = low_lanes(queries.shape)
            zero = jnp.zeros_like(queries)
            outs = []
            for chosen in (jnp.where(low, queries, zero), jnp.where(low, zero, queries)):
                weights = score_weights(chosen, keys[:seen], block * QBLOCK)
                outs.append(mm(weights.astype(bf16), values[:seen]))
            o_ref[here, at] = jnp.where(low_lanes(outs[0].shape), outs[0], outs[1]).astype(bf16)


def attention_backward_kernel(
    qkv_ref, cos_ref, sin_ref, *rest, parts
):
    grad_ref, key_grad, value_grad = rest[-3:]
    do_refs = rest[:parts]
    keys, values = keys_and_values(qkv_ref, cos_ref, sin_ref)
    key_grad[...] = jnp.zeros_like(key_grad)
    value_grad[...] = jnp.zeros_like(value_grad)
    q_cols = do_refs[0].shape[1]
    block_rows = do_refs[0].shape[0]
    for block in range(LEN // QBLOCK):
        here = slice(block * QBLOCK, (block + 1) * QBLOCK)
        seen = (block + 1) * QBLOCK
        for pair in range(q_cols // LANES):
            at = slice(pair * LANES, (pair + 1) * LANES)
            queries = rotated_queries(qkv_ref, cos_ref, sin_ref, here, at)
            inside = block * QBLOCK % block_rows
            out_grad = do_refs[block * QBLOCK // block_rows][inside : inside + QBLOCK, at]
            low = low_lanes(queries.shape)
            zero = jnp.zeros_like(queries)
            parts = []
            for is_low in (True, False):
                q_one = jnp.where(low, queries, zero) if is_low else jnp.where(low, zero, queries)
                g_one = jnp.where(low, out_grad, zero) if is_low else jnp.where(low, zero, out_grad)
                weights = score_weights(q_one, keys[:seen], block * QBLOCK)
                weight_grad = mm(g_one, values[:seen], NT)
                inner = jnp.sum(weights * weight_grad, axis=1, keepdims=True)
                score_grad = (weights * (weight_grad - inner)).astype(bf16)
                parts.append(mm(score_grad, keys[:seen]))
                key_grad[:seen, :] += mm(score_grad, q_one, TN)
                value_grad[:seen, :] += mm(weights.astype(bf16), g_one, TN)
            turned = jnp.where(low_lanes(parts[0].shape), parts[0], parts[1]) * P_SIZE**-0.5
            grad_ref[here, at] = rotated_back(turned, cos_ref[here, :], sin_ref[here, :]).astype(
                bf16
            )
    keys_sum = key_grad[...]
    keys_sum = keys_sum + pltpu.roll(keys_sum, P_SIZE, axis=1)
    values_sum = value_grad[...]
    values_sum = values_sum + pltpu.roll(values_sum, P_SIZE, axis=1)
    keys_sum = rotated_back(keys_sum, cos_ref[...], sin_ref[...])
    grad_ref[:, q_cols:] = jnp.where(low_lanes(keys_sum.shape), keys_sum, values_sum).astype(bf16)


def rotary_tables():
    half = P_SIZE // 2
    frequency = jnp.exp(jnp.arange(half, dtype=f32) * (-2.0 * math.log(rope_base) / P_SIZE))
    angles = jnp.arange(LEN, dtype=f32)[:, None] * frequency[None, :]
    cosine, sine = jnp.cos(angles), jnp.sin(angles)
    return (
        jnp.concatenate([cosine, cosine, cosine, cosine], axis=1),
        jnp.concatenate([-sine, sine, -sine, sine], axis=1),
    )


def short_kernel():
    return pl.CostEstimate(flops=1000, bytes_accessed=1000, transcendentals=0)


def any_place():
    return pl.BlockSpec(memory_space=pl.ANY)


def vmem_params(megabytes):
    return pltpu.CompilerParams(
        vmem_limit_bytes=megabytes * 1024 * 1024, dimension_semantics=("arbitrary",)
    )


def mixer_forward(proj, conv_x, conv_bc, heads, inner_cols, bc_cols):
    rows_all = proj.shape[0]
    states = bc_cols // 2
    bc_at = 2 * inner_cols // bc_cols
    dt_at = (2 * inner_cols + bc_cols) // LANES
    steps = rows_all // CHUNK
    return pl.pallas_call(
        mixer_forward_kernel,
        grid=(steps,),
        in_specs=[
            pl.BlockSpec((CHUNK, inner_cols), lambda i: (i, 0)),
            pl.BlockSpec((CHUNK, inner_cols), lambda i: (i, 1)),
            pl.BlockSpec((CHUNK, bc_cols), lambda i: (i, bc_at)),
            pl.BlockSpec((CHUNK, LANES), lambda i: (i, dt_at)),
            pl.BlockSpec(conv_x.shape, lambda i: (0, 0)),
            pl.BlockSpec(conv_bc.shape, lambda i: (0, 0)),
            pl.BlockSpec(heads.shape, lambda i: (0, 0)),
        ],
        out_specs=[
            pl.BlockSpec((CHUNK, inner_cols), lambda i: (i, 0)),
            pl.BlockSpec((CHUNK, inner_cols), lambda i: (i, 0)),
            pl.BlockSpec((states, inner_cols), lambda i: (i, 0)),
        ],
        out_shape=[
            jax.ShapeDtypeStruct((rows_all, inner_cols), bf16),
            jax.ShapeDtypeStruct((rows_all, inner_cols), bf16),
            jax.ShapeDtypeStruct((steps * states, inner_cols), bf16),
        ],
        scratch_shapes=[
            pltpu.VMEM((states, inner_cols), f32),
            pltpu.VMEM((CHUNK + 8, inner_cols), f32),
            pltpu.VMEM((CHUNK + 8, bc_cols), f32),
        ],
        compiler_params=vmem_params(32),
        cost_estimate=short_kernel(),
        name="mixer_forward",
    )(proj, proj, proj, proj, conv_x, conv_bc, heads)


def mixer_backward(proj, y, dg, held, carry, whole, part, params, inner_cols, bc_cols, *deps):
    rows_all = proj.shape[0]
    states = bc_cols // 2
    bc_at = 2 * inner_cols // bc_cols
    dt_at = (2 * inner_cols + bc_cols) // LANES
    steps = dg.shape[0] // CHUNK
    per = CHUNK // 8
    grad_cols = 2 * inner_cols + bc_cols + LANES

    def at(i):
        return part * steps + steps - 1 - i

    def before(i):
        return jnp.maximum(at(i) * per - 1, 0)

    held_out = [] if whole is None else [whole]
    earlier = held_out + list(deps)
    return pl.pallas_call(
        functools.partial(mixer_backward_kernel, is_start_part=part == 0),
        grid=(steps,),
        in_specs=[
            pl.BlockSpec((CHUNK, inner_cols), lambda i: (at(i), 0)),
            pl.BlockSpec((CHUNK, inner_cols), lambda i: (at(i), 1)),
            pl.BlockSpec((CHUNK, bc_cols), lambda i: (at(i), bc_at)),
            pl.BlockSpec((CHUNK, LANES), lambda i: (at(i), dt_at)),
            pl.BlockSpec((8, inner_cols), lambda i: (before(i), 1)),
            pl.BlockSpec((8, bc_cols), lambda i: (before(i), bc_at)),
            pl.BlockSpec((CHUNK, inner_cols), lambda i: (at(i), 0)),
            pl.BlockSpec((CHUNK, inner_cols), lambda i: (steps - 1 - i, 0)),
            pl.BlockSpec((states, inner_cols), lambda i: (at(i), 0)),
        ]
        + [pl.BlockSpec(value.shape, lambda i: (0, 0)) for value in params]
        + [pl.BlockSpec(carry.shape, lambda i: (0, 0))]
        + [pl.BlockSpec(memory_space=pl.ANY) for _ in earlier],
        out_specs=[
            pl.BlockSpec((CHUNK, grad_cols), lambda i: (at(i), 0)),
            pl.BlockSpec(carry.shape, lambda i: (0, 0)),
        ],
        out_shape=[
            jax.ShapeDtypeStruct((rows_all, grad_cols), bf16),
            jax.ShapeDtypeStruct(carry.shape, f32),
        ],
        scratch_shapes=[
            pltpu.VMEM((CHUNK + 8, inner_cols), f32),
            pltpu.VMEM((CHUNK + 8, bc_cols), f32),
            pltpu.VMEM((CHUNK + 8, inner_cols), f32),
            pltpu.VMEM((CHUNK + 8, bc_cols), f32),
            pltpu.VMEM((HEAD_ROWS, CHUNK), f32),
        ],
        input_output_aliases={14: 0} if held_out else {},
        compiler_params=vmem_params(48),
        cost_estimate=short_kernel(),
        name="mixer_backward",
    )(proj, proj, proj, proj, proj, proj, y, dg, held, *params, carry, *earlier)


def attention_forward(proj, tables, q_cols):
    rows_all = proj.shape[0]
    cols = q_cols + LANES
    return pl.pallas_call(
        attention_forward_kernel,
        grid=(rows_all // LEN,),
        in_specs=[
            pl.BlockSpec((LEN, cols), lambda i: (i, proj.shape[1] // cols - 1)),
            pl.BlockSpec((LEN, LANES), lambda i: (0, 0)),
            pl.BlockSpec((LEN, LANES), lambda i: (0, 0)),
        ],
        out_specs=pl.BlockSpec((LEN, q_cols), lambda i: (i, 0)),
        out_shape=jax.ShapeDtypeStruct((rows_all, q_cols), bf16),
        compiler_params=vmem_params(40),
        cost_estimate=short_kernel(),
        name="attention_forward",
    )(proj, *tables)


def attention_backward(proj, tables, out_grads, q_cols, *deps):
    rows_all = proj.shape[0]
    cols = q_cols + LANES
    return pl.pallas_call(
        functools.partial(attention_backward_kernel, parts=len(out_grads)),
        grid=(rows_all // LEN,),
        in_specs=[
            pl.BlockSpec((LEN, cols), lambda i: (i, proj.shape[1] // cols - 1)),
            pl.BlockSpec((LEN, LANES), lambda i: (0, 0)),
            pl.BlockSpec((LEN, LANES), lambda i: (0, 0)),
        ]
        + [
            pl.BlockSpec((grad.shape[0], q_cols), lambda i: (0, grad.shape[1] // q_cols - 1))
            for grad in out_grads
        ]
        + [any_place() for _ in deps],
        out_specs=pl.BlockSpec((LEN, cols), lambda i: (i, 0)),
        out_shape=jax.ShapeDtypeStruct((rows_all, cols), bf16),
        scratch_shapes=[pltpu.VMEM((LEN, LANES), f32), pltpu.VMEM((LEN, LANES), f32)],
        compiler_params=vmem_params(48),
        cost_estimate=short_kernel(),
        name="attention_backward",
    )(proj, *tables, *out_grads, *deps)


def feed_forward_kernel(
    x_ref, low_ref, arrived_ref, gain_ref, cot_ref, gate_w_ref, up_w_ref, down_w_ref, *rest
):
    mid_ref, n2_ref, act_ref, gate_grad_ref, up_grad_ref, grad_ref, normed, total = rest[-8:]
    step_id = pl.program_id(0)

    @pl.when(step_id == 0)
    def _():
        mid = x_ref[...].astype(f32) + (low_ref[...].astype(f32) + arrived_ref[...].astype(f32))
        inverse = lax.rsqrt(jnp.mean(mid * mid, axis=-1, keepdims=True) + epsilon)
        mid_ref[...] = mid
        value = (mid * inverse * gain_ref[...]).astype(bf16)
        normed[...] = value
        n2_ref[...] = value
        total[...] = jnp.zeros_like(total)

    n2 = normed[...]
    gate = mm(n2, gate_w_ref[...])
    up = mm(n2, up_w_ref[...])
    sig = sigmoid(gate)
    silu = gate * sig
    act_ref[...] = (silu * up).astype(bf16)
    grad = mm(cot_ref[...], down_w_ref[...])
    gate_grad = (grad * up * (sig * (1.0 + gate * (1.0 - sig)))).astype(bf16)
    up_grad = (grad * silu).astype(bf16)
    gate_grad_ref[...] = gate_grad
    up_grad_ref[...] = up_grad
    total[...] += mm(gate_grad, gate_w_ref[...], NT) + mm(up_grad, up_w_ref[...], NT)

    @pl.when(step_id == pl.num_programs(0) - 1)
    def _():
        grad_ref[...] = total[...].astype(bf16)


def feed_forward(tokens, low, arrived, gain, cotangent, w_out, buffers, part, *deps):
    rows, width = low.shape
    hidden = w_out.shape[1] // 3
    blocks = hidden // HIDDEN_BLOCK
    here = pl.BlockSpec((rows, width), lambda h: (part, 0))
    only = pl.BlockSpec((rows, width), lambda h: (0, 0))
    block_out = pl.BlockSpec((rows, HIDDEN_BLOCK), lambda h: (part, h))

    def weight(offset):
        return pl.BlockSpec((width, HIDDEN_BLOCK), lambda h: (0, offset * blocks + h))

    whole = tokens.shape[0]
    return pl.pallas_call(
        feed_forward_kernel,
        grid=(blocks,),
        in_specs=[
            here,
            only,
            only,
            pl.BlockSpec((1, width), lambda h: (0, 0)),
            here,
            weight(0),
            weight(1),
            weight(2),
        ]
        + [any_place() for _ in (*buffers, *deps)],
        out_specs=[here, here, block_out, block_out, block_out, only],
        out_shape=[
            jax.ShapeDtypeStruct((whole, width), f32),
            jax.ShapeDtypeStruct((whole, width), bf16),
            jax.ShapeDtypeStruct((whole, hidden), bf16),
            jax.ShapeDtypeStruct((whole, hidden), bf16),
            jax.ShapeDtypeStruct((whole, hidden), bf16),
            jax.ShapeDtypeStruct((rows, width), bf16),
        ],
        scratch_shapes=[pltpu.VMEM((rows, width), bf16), pltpu.VMEM((rows, width), f32)],
        input_output_aliases={8 + i: i for i in range(len(buffers))},
        compiler_params=vmem_params(40),
        cost_estimate=short_kernel(),
        name="feed_forward",
    )(tokens, low, arrived, gain, cotangent, w_out, w_out, w_out, *buffers, *deps)


def branch_grad_kernel(mid_ref, low_ref, arrived_ref, gain_ref, cot_ref, w_ref, *rest):
    hidden_ref, branch_ref, mix_ref = rest[-3:]
    mid = mid_ref[...]
    inverse = lax.rsqrt(jnp.mean(mid * mid, axis=-1, keepdims=True) + epsilon)
    unit = mid * inverse
    low = low_ref[...].astype(f32)
    scaled = (low + arrived_ref[...].astype(f32)) * gain_ref[...]
    inner = jnp.mean(scaled * unit, axis=-1, keepdims=True)
    grad = cot_ref[...].astype(f32) + (scaled - unit * inner) * inverse
    hidden_ref[...] = grad
    rounded = grad.astype(bf16)
    branch_ref[...] = rounded
    mix_ref[...] = mm(rounded, w_ref[...]).astype(bf16)


def branch_grad(mid, low, arrived, gain, cotangent, w_in, buffers, part, *deps):
    rows, width = low.shape
    whole = cotangent.shape[0]
    mix_cols = width
    here = pl.BlockSpec((rows, width), lambda i: (part, 0))
    only = pl.BlockSpec((rows, width), lambda i: (0, 0))
    row = pl.BlockSpec((1, width), lambda i: (0, 0))
    return pl.pallas_call(
        branch_grad_kernel,
        grid=(1,),
        in_specs=[here, only, only, row, here, pl.BlockSpec(w_in.shape, lambda i: (0, 0))]
        + [any_place() for _ in (*buffers, *deps)],
        out_specs=[here, here, pl.BlockSpec((rows, mix_cols), lambda i: (0, 0))],
        out_shape=[
            jax.ShapeDtypeStruct((whole, width), f32),
            jax.ShapeDtypeStruct((whole, width), bf16),
            jax.ShapeDtypeStruct((rows, mix_cols), bf16),
        ],
        input_output_aliases={6 + i: i for i in range(len(buffers))},
        compiler_params=vmem_params(32),
        cost_estimate=short_kernel(),
        name="branch_grad",
    )(mid, low, arrived, gain, cotangent, w_in, *buffers, *deps)


def weight_grad_kernel(left_ref, right_ref, *rest, has_arrived):
    total = mm(left_ref[...], right_ref[...])
    if has_arrived:
        total = (total + rest[0][...].astype(f32)).astype(bf16)
        rows = total.shape[0] // 2
        rest[-2][...] = total[:rows]
        rest[-1][...] = total[rows:]
    else:
        rest[-1][...] = total.astype(bf16)


def weight_grad(
    left, half, right, right_start, right_cols, buffers, start, columns, arrived, deps
):
    block = 384 if right_cols % 384 == 0 else 256
    offset = right_start // block
    rows, tokens = left.shape
    if half is not None:
        rows //= 2
    first = start // block
    extra = [] if arrived is None else [arrived]
    outs = 1 + len(extra)
    return pl.pallas_call(
        functools.partial(weight_grad_kernel, has_arrived=arrived is not None),
        grid=(right_cols // block,),
        in_specs=[
            pl.BlockSpec((rows, tokens), lambda n: (half or 0, 0)),
            pl.BlockSpec((tokens, block), lambda n: (0, offset + n)),
        ]
        + [pl.BlockSpec((rows, block), lambda n: (0, first + n)) for _ in extra]
        + [any_place() for _ in (*buffers, *deps)],
        out_specs=[pl.BlockSpec((rows // outs, block), lambda n: (0, first + n))] * outs,
        out_shape=[jax.ShapeDtypeStruct((rows // outs, columns), bf16)] * outs,
        input_output_aliases={2 + len(extra) + i: i for i in range(len(buffers))},
        compiler_params=vmem_params(24),
        cost_estimate=short_kernel(),
        name="weight_grad",
    )(left, right, *extra, *buffers, *deps)


def whole(left, right):
    return left, right, 0, right.shape[1]


def weight_grads(pieces, half, arrived=None, deps=(), late=()):
    columns = sum(piece[3] for piece in pieces)
    buffers, start = (), 0
    for left, right, right_start, right_cols in pieces:
        buffers = weight_grad(
            left, half, right, right_start, right_cols, buffers, start, columns, arrived, deps
        )
        deps, late = late, ()
        start += right_cols
    return buffers[0] if arrived is None else buffers


def product_kernel(*refs, count):
    total = mm(refs[0][...], refs[count][...], NT)
    for i in range(1, count):
        total = total + mm(refs[i][...], refs[count + i][...], NT)
    refs[-1][...] = total.astype(bf16)


def product(pairs, *deps):
    rows, out_cols = pairs[0][0].shape[0], pairs[0][1].shape[0]
    block = 256
    return pl.pallas_call(
        functools.partial(product_kernel, count=len(pairs)),
        grid=(out_cols // block,),
        in_specs=[pl.BlockSpec(left.shape, lambda i: (0, 0)) for left, _, _ in pairs]
        + [
            pl.BlockSpec((block, left.shape[1]), lambda i, at=at: (i, at))
            for left, _, at in pairs
        ]
        + [any_place() for _ in deps],
        out_specs=pl.BlockSpec((rows, block), lambda i: (0, i)),
        out_shape=jax.ShapeDtypeStruct((rows, out_cols), bf16),
        compiler_params=vmem_params(32),
        cost_estimate=short_kernel(),
        name="product",
    )(*[left for left, _, _ in pairs], *[right for _, right, _ in pairs], *deps)


def halves_kernel(side_ref, *refs, count):
    total = mm(refs[0][...], refs[count][...], NT)
    for i in range(1, count):
        total = total + mm(refs[i][...], refs[count + i][...], NT)
    there_ref, own_ref, held = refs[-3:]
    held[...] = total.astype(bf16)
    rows = there_ref.shape[0]
    other = pl.multiple_of((1 - side_ref[0]) * rows, rows)
    there_ref[...] = held[pl.ds(other, rows), :]
    own_ref[...] = held[pl.ds(pl.multiple_of(side_ref[0] * rows, rows), rows), :]


def product_halves(side, pairs, *deps):
    rows, out_cols = pairs[0][0].shape[0], pairs[0][1].shape[0]
    block = 256
    return pl.pallas_call(
        functools.partial(halves_kernel, count=len(pairs)),
        grid=(out_cols // block,),
        in_specs=[pl.BlockSpec(memory_space=pltpu.SMEM)]
        + [pl.BlockSpec(left.shape, lambda i: (0, 0)) for left, _, _ in pairs]
        + [
            pl.BlockSpec((block, left.shape[1]), lambda i, at=at: (i, at))
            for left, _, at in pairs
        ]
        + [any_place() for _ in deps],
        out_specs=[pl.BlockSpec((rows // 2, block), lambda i: (0, i))] * 2,
        out_shape=[jax.ShapeDtypeStruct((rows // 2, out_cols), bf16)] * 2,
        scratch_shapes=[pltpu.VMEM((rows, block), bf16)],
        compiler_params=vmem_params(32),
        cost_estimate=short_kernel(),
        name="product_halves",
    )(side, *[left for left, _, _ in pairs], *[right for _, right, _ in pairs], *deps)


def layer_out_kernel(side_ref, mid_ref, own_ref, there_ref, *rest):
    total = own_ref[...].astype(f32) + there_ref[...].astype(f32)
    rest[-1][...] = (mid_ref[...] + total).astype(bf16)


def input_grad_kernel(side_ref, grad_ref, own_ref, there_ref, x_ref, gain_ref, *rest):
    x = x_ref[...].astype(f32)
    inverse = lax.rsqrt(jnp.mean(x * x, axis=-1, keepdims=True) + epsilon)
    unit = x * inverse
    scaled = (own_ref[...].astype(f32) + there_ref[...].astype(f32)) * gain_ref[...]
    inner = jnp.mean(scaled * unit, axis=-1, keepdims=True)
    rest[-1][...] = (grad_ref[...] + (scaled - unit * inner) * inverse).astype(bf16)


def own_rows(kernel, side, whole_parts, parts, row, deps):
    rows, columns = parts[0].shape
    block = 128
    steps = rows // block
    here = pl.BlockSpec((block, columns), lambda i, side: (i, 0))
    mine = pl.BlockSpec((block, columns), lambda i, side: (side[0] * steps + i, 0))
    return pl.pallas_call(
        kernel,
        grid_spec=pltpu.PrefetchScalarGridSpec(
            num_scalar_prefetch=1,
            grid=(steps,),
            in_specs=[mine for _ in whole_parts]
            + [here for _ in parts]
            + [pl.BlockSpec(value.shape, lambda i, side: (0, 0)) for value in row]
            + [any_place() for _ in deps],
            out_specs=here,
        ),
        out_shape=jax.ShapeDtypeStruct((rows, columns), bf16),
        compiler_params=vmem_params(24),
        cost_estimate=short_kernel(),
        name="own_rows",
    )(side, *whole_parts, *parts, *row, *deps)


def inverse_rms(values):
    return lax.rsqrt(jnp.mean(values * values, axis=-1, keepdims=True) + epsilon)


def swap_tensor(values):
    return lax.ppermute(values, "tensor", [(0, 1), (1, 0)])


def swap_dp(values, bit):
    return lax.ppermute(values, "dp", [(i, i ^ bit) for i in range(lax.axis_size("dp"))])


def both_halves(mine):
    other = swap_tensor(mine)
    return jnp.where(
        lax.axis_index("tensor") == 0,
        jnp.concatenate([mine, other], axis=0),
        jnp.concatenate([other, mine], axis=0),
    )


def half_rows(values, index):
    rows = values.shape[0] // 2
    return lax.dynamic_slice_in_dim(values, index * rows, rows, 0)


def after(values, *earlier):
    return pl.pallas_call(
        lambda *refs: None,
        in_specs=[any_place()] * (1 + len(earlier)),
        out_specs=any_place(),
        out_shape=jax.ShapeDtypeStruct(values.shape, values.dtype),
        input_output_aliases={0: 0},
        cost_estimate=short_kernel(),
        name="after",
    )(values, *earlier)


def swap_tensor(values):
    return lax.ppermute(values, "tensor", [(0, 1), (1, 0)])


def swap_dp(values, bit):
    return lax.ppermute(values, "dp", [(i, i ^ bit) for i in range(lax.axis_size("dp"))])


def both_halves(mine):
    other = swap_tensor(mine)
    return jnp.where(
        lax.axis_index("tensor") == 0,
        jnp.concatenate([mine, other], axis=0),
        jnp.concatenate([other, mine], axis=0),
    )


def half_rows(values, index):
    rows = values.shape[0] // 2
    return lax.dynamic_slice_in_dim(values, index * rows, rows, 0)


def chosen_half(parts, index):
    middle = len(parts) // 2
    return jnp.where(
        index == 0,
        jnp.concatenate(parts[:middle], axis=0),
        jnp.concatenate(parts[middle:], axis=0),
    )


def after(values, *earlier):
    return pl.pallas_call(
        lambda *refs: None,
        in_specs=[any_place()] * (1 + len(earlier)),
        out_specs=any_place(),
        out_shape=jax.ShapeDtypeStruct(values.shape, values.dtype),
        input_output_aliases={0: 0},
        cost_estimate=short_kernel(),
        name="after",
    )(values, *earlier)


def sum_far_kernel(own_ref, arrived_ref, *rest):
    rest[-1][...] = (own_ref[...].astype(f32) + arrived_ref[...].astype(f32)).astype(bf16)


def reordering(width):
    dp_count = lax.axis_size("dp")
    here = width // dp_count
    me = lax.axis_index("dp")
    core, near = lax.rem(me, 2), lax.rem(lax.div(me, 2), 2)
    place = jnp.arange(width, dtype=jnp.int32)
    block, inside = place // here, place % here
    quarter, far = block // (dp_count // 4), block % (dp_count // 4)
    block_core = jnp.where(quarter // 2 == 0, 1 - core, core)
    block_near = jnp.where(quarter % 2 == 0, 1 - near, near)
    source = (far * 4 + block_near * 2 + block_core) * here + inside
    return (source[:, None] == jnp.arange(width, dtype=jnp.int32)[None, :]).astype(bf16)


def sum_near(halves):
    there, own = halves
    return own, swap_dp(there, 2)


def sum_far_kernel(me_ref, own_ref, arrived_ref, *rest, far):
    total = (own_ref[...].astype(f32) + arrived_ref[...].astype(f32)).astype(bf16)
    rows = total.shape[0] // far
    scratch = rest[-1]
    scratch[...] = total
    for offset, out_ref in enumerate(rest[-1 - far : -1]):
        place = lax.rem(me_ref[0] + offset, far)
        out_ref[...] = scratch[pl.ds(pl.multiple_of(place * rows, rows), rows), :]


def sum_far(own, arrived, *deps):
    far = lax.axis_size("dp") // 4
    if far > 4:
        return (after((own.astype(f32) + arrived.astype(f32)).astype(bf16), *deps),)
    rows, columns = own.shape
    me = lax.div(lax.axis_index("dp"), 4).reshape(1)
    only = pl.BlockSpec((rows, columns), lambda i: (0, 0))
    return pl.pallas_call(
        functools.partial(sum_far_kernel, far=far),
        grid=(1,),
        in_specs=[pl.BlockSpec(memory_space=pltpu.SMEM), only, only]
        + [any_place() for _ in deps],
        out_specs=[pl.BlockSpec((rows // far, columns), lambda i: (0, 0))] * far,
        out_shape=[jax.ShapeDtypeStruct((rows // far, columns), bf16)] * far,
        scratch_shapes=[pltpu.VMEM((rows, columns), bf16)],
        compiler_params=vmem_params(24),
        cost_estimate=short_kernel(),
        name="sum_far",
    )(me, own, arrived, *deps)


def send_far(blocks):
    far = lax.axis_size("dp") // 4
    if far > 4:
        groups = [[low + 4 * i for i in range(far)] for low in range(4)]
        summed = blocks[0].reshape(far, blocks[0].shape[0] // far, blocks[0].shape[1])
        return [lax.all_to_all(summed, "dp", 0, 0, tiled=True, axis_index_groups=groups)]
    arrived = []
    for offset in range(1, far):
        moves = [(i, (i + 4 * offset) % (4 * far)) for i in range(4 * far)]
        arrived.append(lax.ppermute(blocks[offset], "dp", moves))
    return arrived


def sum_last(blocks, arrived, *deps):
    if arrived[0].ndim == 3:
        return jnp.sum(after(arrived[0], *deps).astype(f32), axis=0)
    total = after(blocks[0], *deps, *arrived).astype(f32)
    for values in arrived:
        total = total + values.astype(f32)
    return total


def add_kernel(left_ref, right_ref, *rest):
    rest[-1][...] = left_ref[...] + right_ref[...]


def added(left, right, *deps):
    only = pl.BlockSpec(left.shape, lambda i: (0, 0))
    return pl.pallas_call(
        add_kernel,
        grid=(1,),
        in_specs=[only, only] + [any_place() for _ in deps],
        out_specs=only,
        out_shape=jax.ShapeDtypeStruct(left.shape, left.dtype),
        compiler_params=vmem_params(16),
        cost_estimate=short_kernel(),
        name="added",
    )(left, right, *deps)


def local(
    tokens,
    gains,
    w_zx,
    w_bc,
    w_dt,
    conv_x,
    conv_bc,
    head_params,
    w_mo,
    w_q,
    w_kv,
    w_ao,
    w_gu,
    w_down,
    cotangent,
):
    dp_count = lax.axis_size("dp")
    side = lax.axis_index("tensor")
    width = tokens.shape[1]
    here = width // dp_count
    inner_cols, bc_cols, head_cols = w_zx.shape[2], w_bc.shape[1], w_dt.shape[1]
    q_cols, kv_cols = w_q.shape[1], 2 * w_kv.shape[2]
    hidden, mo_cols, ao_cols = w_gu.shape[2], w_mo.shape[0], w_ao.shape[0]
    bc_start = 2 * inner_cols
    dt_start = bc_start + bc_cols
    q_start = dt_start + LANES
    kv_start = q_start + q_cols
    in_cols = kv_start + kv_cols

    shared = both_halves(jnp.concatenate([w_bc, gains.T], axis=1))
    in_pack = jnp.concatenate(
        [
            w_zx[:, 0],
            w_zx[:, 1],
            shared[:, :bc_cols],
            w_dt,
            shared[:, bc_cols:],
            jnp.zeros((here, LANES - head_cols - 2), bf16),
            w_q,
            w_kv.reshape(here, kv_cols),
            w_mo.T,
            w_ao.T,
        ],
        axis=1,
    )
    w_in = lax.all_gather(in_pack, "dp", axis=0, tiled=True)
    out_pack = jnp.concatenate([w_gu.reshape(here, 2 * hidden), w_down.T], axis=1)
    tokens_all = both_halves(tokens)
    cotangent_all = both_halves(cotangent)
    out_pack = after(out_pack, w_in, tokens_all, cotangent_all)
    w_out = lax.all_gather(out_pack, "dp", axis=0, tiled=True)
    tables = rotary_tables()
    order = reordering(width)
    unchanged = jnp.eye(width, dtype=bf16)
    kept_rows = width // 2

    mix_full = w_in[:, in_cols:]
    gain_full = w_in[:, dt_start + head_cols : dt_start + head_cols + 2].T.astype(f32)
    gain_one, gain_two = gain_full[0:1], gain_full[1:2]
    heads = jnp.pad(head_params, ((0, 5), (0, LANES - head_cols)))
    mixer_params = (conv_x, conv_bc, heads, heads[:, :HEAD_ROWS].T)

    seq_in = tokens_all.astype(f32)
    inverse_one = inverse_rms(seq_in)
    n1 = (seq_in * inverse_one * gain_one).astype(bf16)
    proj = mm(n1, w_in[:, :in_cols])
    gated, y, held = mixer_forward(proj, conv_x, conv_bc, heads, inner_cols, bc_cols)
    attended = attention_forward(proj, tables, q_cols)

    rows = tokens_all.shape[0] // ROW_PARTS
    backward_parts = list(range(ROW_PARTS))[::-1]
    branch_low, branch_arrived = {}, {}
    for part in backward_parts:
        at = slice(part * rows, (part + 1) * rows)
        branch_low[part] = (
            mm(gated[at], mix_full[:, :mo_cols], NT) + mm(attended[at], mix_full[:, mo_cols:], NT)
        ).astype(bf16)
        branch_arrived[part] = swap_tensor(branch_low[part])
    n1_ordered = product([(order, n1, 0)])
    cotangent_turned = product([(unchanged, cotangent_all, 0)])
    start = backward_parts[0]
    ready = (n1_ordered, cotangent_turned, mix_full)

    n2_grad_low, n2_grad_arrived = {}, {}
    buffers = ()
    for part in backward_parts:
        *buffers, grad_low = feed_forward(
            tokens_all,
            branch_low[part],
            branch_arrived[part],
            gain_two,
            cotangent_all,
            w_out,
            buffers,
            part,
            *ready,
        )
        ready = ()
        n2_grad_low[part] = grad_low
        n2_grad_arrived[part] = swap_tensor(grad_low)
    hidden_one, n2, activated, gate_grad, up_grad = buffers
    n2_turned = product([(unchanged, n2, 0)])
    ffn_pieces = [
        whole(n2_turned, gate_grad),
        whole(n2_turned, up_grad),
        whole(cotangent_turned, activated),
    ]
    ffn_all = weight_grads(ffn_pieces, None, late=(n2_grad_arrived[start],))
    ffn_sum = lax.psum_scatter(ffn_all, "dp", scatter_dimension=0, tiled=True)

    mix_grad = {}
    buffers, proj_grad = (), None
    carry = jnp.zeros((bc_cols // 2 + 32 + 2 * HEAD_ROWS, inner_cols), f32)
    step = ffn_all
    last = backward_parts[-1]
    for part in backward_parts:
        *buffers, mix_grad[part] = branch_grad(
            hidden_one,
            n2_grad_low[part],
            n2_grad_arrived[part],
            gain_two,
            cotangent_all,
            mix_full,
            buffers,
            part,
            step,
        )
        deps = ()
        if part == last:
            ffn_low = product([(activated, w_out, 2)], buffers[1])
            ffn_there = swap_tensor(half_rows(ffn_low, 1 - side))
            branch_ordered = product([(order, buffers[1], 0)], ffn_low)
            mix_pieces = [whole(branch_ordered, gated), whole(branch_ordered, attended)]
            mix_sent = weight_grads(mix_pieces, 0)
            mix_arrived = swap_dp(mix_sent, 1)
            out_grads = [mix_grad[each] for each in range(ROW_PARTS)]
            att_grad = attention_backward(proj, tables, out_grads, q_cols, mix_sent)
            att_pieces = [whole(n1_ordered, att_grad)]
            att_sent = weight_grads(att_pieces, 0)
            att_arrived = swap_dp(att_sent, 1)
            mix_near = sum_near(weight_grads(mix_pieces, 1, mix_arrived, (att_sent,)))
            att_near = sum_near(weight_grads(att_pieces, 1, att_arrived, (mix_near[0],)))
            deps = (att_near[0], ffn_there)
        proj_grad, carry = mixer_backward(
            proj,
            y,
            mix_grad[part],
            held,
            carry,
            proj_grad,
            part,
            mixer_params,
            inner_cols,
            bc_cols,
            *deps,
        )

    sums = carry[bc_cols // 2 + 8 :]
    sums_arrived = swap_dp(sums, 1)
    mix_step = sum_far(*mix_near, carry)
    mix_far = send_far(mix_step)
    att_step = sum_far(*att_near, mix_step[0])
    att_far = send_far(att_step)
    wide_cols = inner_cols + inner_cols // 2
    second_cols = q_start - wide_cols
    first_pieces = [(n1_ordered, proj_grad, 0, wide_cols)]
    second_pieces = [(n1_ordered, proj_grad, wide_cols, second_cols)]
    first_sent = weight_grads(first_pieces, 0, deps=(att_step[0],))
    first_arrived = swap_dp(first_sent, 1)
    second_sent = weight_grads(second_pieces, 0, deps=(first_sent,))
    second_arrived = swap_dp(second_sent, 1)
    sums = added(sums, sums_arrived, second_sent)
    sums_arrived = swap_dp(sums, 2)
    first_near = sum_near(weight_grads(first_pieces, 1, first_arrived, (sums,)))
    second_near = sum_near(weight_grads(second_pieces, 1, second_arrived, (first_near[0],)))
    n1_there, n1_own = product_halves(
        side.reshape(1),
        [(proj_grad, w_in, 0), (att_grad, w_in, q_start // (in_cols - q_start))],
        second_near[0],
        *mix_far,
        *att_far,
    )
    n1_arrived = swap_tensor(n1_there)
    sums = added(sums, sums_arrived, n1_own)
    sums_arrived = swap_dp(sums, 4)
    first_step = sum_far(*first_near, n1_own)
    first_far = send_far(first_step)
    sums = added(sums, sums_arrived, first_step[0])
    bit = 8
    while bit < dp_count // 2:
        sums = added(sums, swap_dp(sums, bit))
        bit *= 2
    sums_arrived = swap_dp(sums, bit)
    layer_out = own_rows(
        layer_out_kernel, side.reshape(1), [hidden_one, ffn_low], [ffn_there], [], first_far[:1]
    )
    second_step = sum_far(*second_near, sums, layer_out, *first_far)
    second_far = send_far(second_step)
    sums = added(sums, sums_arrived, second_step[0])
    input_grad = own_rows(
        input_grad_kernel,
        side.reshape(1),
        [buffers[0]],
        [n1_own, n1_arrived, tokens],
        [gain_one],
        [second_step[0]],
    )
    ffn_sum = after(ffn_sum, input_grad, *second_far).astype(f32)
    mix_sum = sum_last(mix_step, mix_far, input_grad, *second_far)
    att_sum = sum_last(att_step, att_far, input_grad, *second_far)
    first_sum = sum_last(first_step, first_far, input_grad, *second_far)
    second_sum = sum_last(second_step, second_far, input_grad)

    taps = conv_x.shape[0]
    grad_conv_x = sums[:taps]
    conv_bc_half = sums[16 : 16 + taps, :bc_cols]
    head_sums = jnp.sum(sums[24:, :CHUNK], axis=1)
    grad_head = jnp.stack(
        [
            head_sums[:head_cols],
            head_sums[HEAD_ROWS : HEAD_ROWS + head_cols],
            jnp.sum(sums[taps].reshape(head_cols, P_SIZE), axis=1),
        ]
    )

    in_low = after(in_pack, input_grad).astype(f32)
    gain_one_grad = (
        jnp.sum(in_low[:, :wide_cols] * first_sum, axis=1)
        + jnp.sum(in_low[:, wide_cols:q_start] * second_sum[:, :second_cols], axis=1)
        + jnp.sum(in_low[:, q_start:in_cols] * att_sum, axis=1)
    ) / shared[:, bc_cols].astype(f32)
    gain_two_grad = jnp.sum(
        out_pack[:, : 2 * hidden].astype(f32) * ffn_sum[:, : 2 * hidden], axis=1
    ) / shared[:, bc_cols + 1].astype(f32)
    shared_half = jnp.concatenate(
        [
            second_sum[:, bc_start - wide_cols : dt_start - wide_cols],
            jnp.stack([gain_one_grad, gain_two_grad], axis=1),
        ],
        axis=1,
    )
    to_send = jnp.concatenate(
        [half_rows(shared_half, 1 - side).reshape(-1), conv_bc_half.reshape(-1)]
    )
    arrived = swap_tensor(to_send)
    shared_sum = half_rows(shared_half, side) + arrived[: shared_half.size // 2].reshape(
        here // 2, bc_cols + 2
    )
    grad_conv_bc = conv_bc_half + arrived[shared_half.size // 2 :].reshape(taps, bc_cols)
    return (
        layer_out,
        input_grad,
        shared_sum[:, bc_cols:].T,
        jnp.concatenate([first_sum, second_sum[:, : bc_start - wide_cols]], axis=1).reshape(
            here, 2, inner_cols
        ),
        shared_sum[:, :bc_cols],
        second_sum[:, dt_start - wide_cols : dt_start - wide_cols + head_cols],
        grad_conv_x,
        grad_conv_bc,
        grad_head,
        mix_sum[:, :mo_cols].T,
        att_sum[:, :q_cols],
        att_sum[:, q_cols:].reshape(here, 2, kv_cols // 2),
        mix_sum[:, mo_cols:].T,
        ffn_sum[:, : 2 * hidden].reshape(here, 2, hidden),
        ffn_sum[:, 2 * hidden :].T,
    )


def solution(mesh):
    placed = (
        P(("dp", "tensor"), None),
        P(None, ("dp", "tensor")),
        P("dp", None, "tensor"),
        P(("dp", "tensor"), None),
        P("dp", "tensor"),
        P(None, "tensor"),
        P(),
        P(None, "tensor"),
        P("tensor", "dp"),
        P("dp", "tensor"),
        P("dp", None, "tensor"),
        P("tensor", "dp"),
        P("dp", None, "tensor"),
        P("tensor", "dp"),
        P(("dp", "tensor"), None),
    )
    return jax.shard_map(
        local,
        mesh=mesh,
        in_specs=placed,
        out_specs=(
            P(("dp", "tensor"), None),
            P(("dp", "tensor"), None),
            P(None, ("dp", "tensor")),
            P("dp", None, "tensor"),
            P(("dp", "tensor"), None),
            P("dp", "tensor"),
            P(None, "tensor"),
            P(),
            P(None, "tensor"),
            P("tensor", "dp"),
            P("dp", "tensor"),
            P("dp", None, "tensor"),
            P("tensor", "dp"),
            P("dp", None, "tensor"),
            P("tensor", "dp"),
        ),
        check_vma=False,
    )
```
